128 devices in a mesh: rep: 8 (over z, core), shard: 16 (over y, x).
Axes of the slice: x: 4, y: 4, z: 4, core: 2. Of those that a mesh axis runs over, the one named last changes fastest.
Arguments:
- partials: bfloat16 [8, 48, 1024, 1024], P('rep', None, 'shard'), may hold values from -2.5 to 2.5
- owned_block: int32 [128], replicated, may hold values from -1 to 47, as said below
Outputs:
- directions: bfloat16 [48, 1024, 1024], P(None, 'shard')
The draws below stay inside these ranges and needn't reach their ends.
Inputs may be any that keep to these rules, and one draw needn't show every extreme that they name: `owned_block`: exactly 42 entries name a block, no block is named twice, every other entry is -1.
All inputs are finite; a program needn't handle non-finite values.
Results may differ from the reference program's by a relative error of at most 0.014.
Values may be sent and summed in bfloat16 or wider, within the bound.
No kernel may reach another device: no remote copies, remote signals or barrier semaphores. Data moves between devices by JAX's collectives and lax.ppermute only.
A program may use at most 128 MiB of HBM per device.

```python
import jax
import jax.numpy as jnp
from jax import lax

BS = 1024
ITERS = 2
NB = 48
ACTIVE = 42
N_REP = 8
N_SHARD = 16


def draw_owned_block(key, part):
    key = jax.random.fold_in(key, 11)
    slot_key, block_key = jax.random.split(key)
    slots = jax.random.permutation(slot_key, N_REP * N_SHARD).astype(jnp.int32)
    order = jax.random.permutation(block_key, NB).astype(jnp.int32)
    leading = order[0]
    order = jnp.where(order == NB - 1, leading, order)
    order = order.at[0].set(NB - 1)
    owned = jnp.full((N_REP * N_SHARD,), -1, jnp.int32)
    return owned.at[slots[:ACTIVE]].set(order[:ACTIVE])


def block_levels(stream_key, shape, pieces, smallest, high):
    def one(axis_at, shards_of):
        steps = jax.random.uniform(jax.random.fold_in(jax.random.fold_in(stream_key, 6), axis_at), (shards_of,), jnp.float32, smallest / len(pieces), high / len(pieces))
        return jnp.repeat(jnp.exp(steps), shape[axis_at] // shards_of).reshape((-1,) + (1,) * (len(shape) - axis_at - 1))

    level = one(*pieces[0])
    for cut in pieces[1:]:
        level = level * one(*cut)
    return level


def bell_draw(stream_key, shape, scale, reach, shards=(), kind=jnp.bfloat16):
    array = scale * jax.random.normal(stream_key, shape, jnp.float32)
    if shards:
        array = array * block_levels(stream_key, shape, shards, -0.22, 0.18)
    return jnp.clip(array, -reach, reach).astype(kind)


def setup_inputs(seed: int = 0) -> dict:
    splits = jax.random.split(jax.random.key(seed), 3)
    return {
        "partials": bell_draw(splits[0], (N_REP, NB, BS, BS), 0.35, 2.5, ((0, 8), (2, 16))),
        "owned_block": draw_owned_block(jax.random.fold_in(splits[2], 71), 0),
    }


damping = 0.1

def inverse_root(statistic):
    width = statistic.shape[0]
    identity = jnp.eye(width, dtype=jnp.float32)
    norm_scale = 0.25 * jnp.sqrt(jnp.sum(statistic * statistic))
    coupled = (statistic / norm_scale).astype(jnp.bfloat16)
    factor_step = ((5.0 * identity - coupled.astype(jnp.float32)) * 0.25).astype(jnp.bfloat16)
    root_now = factor_step
    for turn in range(ITERS - 1):
        step_square = jnp.dot(factor_step, factor_step, preferred_element_type=jnp.float32).astype(jnp.bfloat16)
        step_fourth = jnp.dot(step_square, step_square, preferred_element_type=jnp.float32).astype(jnp.bfloat16)
        coupled = jnp.dot(step_fourth, coupled, preferred_element_type=jnp.float32).astype(jnp.bfloat16)
        factor_step = ((5.0 * identity - coupled.astype(jnp.float32)) * 0.25).astype(jnp.bfloat16)
        root_now = jnp.dot(root_now, factor_step, preferred_element_type=jnp.float32).astype(jnp.bfloat16)
    return root_now

def precondition(gradient):
    width = gradient.shape[0]
    identity = jnp.eye(width, dtype=jnp.float32)
    left = jnp.dot(gradient, gradient.T, preferred_element_type=jnp.float32) / width + damping * identity
    right = jnp.dot(gradient.T, gradient, preferred_element_type=jnp.float32) / width + damping * identity
    left_root = inverse_root(left)
    right_root = inverse_root(right)
    left_side = jnp.dot(left_root, gradient, preferred_element_type=jnp.float32).astype(jnp.bfloat16)
    raw_dir = jnp.dot(left_side, right_root, preferred_element_type=jnp.float32)
    grad_values = gradient.astype(jnp.float32)
    graft_ratio = jnp.sqrt(jnp.mean(grad_values * grad_values) + 1e-06) / jnp.sqrt(jnp.mean(raw_dir * raw_dir) + 1e-06)
    return (raw_dir * graft_ratio).astype(jnp.bfloat16)

def reference(partials, owned_block):
    summed = partials[0].astype(jnp.float32)
    for replica in range(1, N_REP):
        summed = summed + partials[replica].astype(jnp.float32)
    grad = summed.astype(jnp.bfloat16)
    active_ids = jnp.sort(owned_block)[N_REP * N_SHARD - ACTIVE:].astype(jnp.int32)
    directions = lax.map(precondition, grad[active_ids])
    return grad.at[active_ids].set(directions)
```

```python
import functools

import jax
import jax.numpy as jnp
from jax import lax
from jax.experimental import pallas as pl
from jax.experimental.pallas import tpu as pltpu
from jax.sharding import Mesh, PartitionSpec as P

damping = 0.1
mib = 2**20
ROWS = ((0,), (0,))
COLUMNS = ((1,), (1,))


def dot(a, b, contract=((1,), (0,))):
    return lax.dot_general(a, b, (contract, ((), ())), preferred_element_type=jnp.float32)


def rows_at(start, count):
    return pl.ds(pl.multiple_of(start, count), count)


def root_kernel(place, own, sibling, root, grad, stat, step, square, coupled):
    core = place[0]
    half, width = own.shape
    grad[rows_at(core * half, half), :] = own[...]
    grad[rows_at((1 - core) * half, half), :] = sibling[...]
    low, high = slice(0, half), slice(half, width)
    upper = ((low, low), (low, high), (high, high))
    eye = lax.broadcasted_iota(jnp.int32, (half, half), 0) == lax.broadcasted_iota(
        jnp.int32, (half, half), 1
    )

    def statistic(contract):
        total = jnp.zeros((1, half), jnp.float32)
        for r, c in upper:
            if contract == ROWS:
                product = dot(grad[:, r], grad[:, c], ROWS)
            else:
                product = dot(grad[r, :], grad[c, :], COLUMNS)
            value = product * (1.0 / width)
            if r == c:
                value = value + jnp.where(eye, damping, 0.0)
            stat[r, c] = value
            squares = jnp.sum(value * value, axis=0, keepdims=True)
            total = total + (squares if r == c else 2.0 * squares)
        return total

    total = lax.cond(core == 0, lambda: statistic(COLUMNS), lambda: statistic(ROWS))
    inverse = 4.0 * lax.rsqrt(jnp.sum(total, axis=1, keepdims=True))
    across, along = {}, {}
    for r, c in upper:
        matrix = (stat[r, c] * inverse).astype(jnp.bfloat16).astype(jnp.float32)
        if r == c:
            value = ((jnp.where(eye, 5.0, 0.0) - matrix) * 0.25).astype(jnp.bfloat16)
            both = jnp.where(eye, 4.0 * value.astype(jnp.float32) + matrix, 0.0)
            across[r.start] = jnp.sum(both, axis=0, keepdims=True)
            along[r.start] = jnp.sum(both, axis=1, keepdims=True)
        else:
            value = (matrix * -0.25).astype(jnp.bfloat16)
        step[r, c] = value

    def times_itself(matrix):
        one, two, three = (matrix[block] for block in upper)
        yield upper[0], dot(one, one) + dot(two, two, COLUMNS)
        yield upper[1], dot(one, two) + dot(two, three)
        yield upper[2], dot(two, two, ROWS) + dot(three, three)

    for (r, c), product in times_itself(step):
        square[r, c] = product.astype(jnp.bfloat16)
        value = step[r, c].astype(jnp.float32)
        coupled[r, c] = (value * across[c.start] - 4.0 * product).astype(jnp.bfloat16)
        if r != c:
            coupled[high, low] = (value * along[r.start] - 4.0 * product).astype(jnp.bfloat16)
    one, two, three = (product.astype(jnp.bfloat16) for _, product in times_itself(square))
    products = (
        dot(one, coupled[low, low]) + dot(two, coupled[high, low], COLUMNS),
        dot(one, coupled[low, high]) + dot(two, coupled[high, high]),
        dot(two, coupled[low, high], ROWS) + dot(three, coupled[high, high]),
    )
    for (r, c), product in zip(upper, products):
        value = ((5.0 * step[r, c].astype(jnp.float32) - product) * 0.25).astype(jnp.bfloat16)
        root[upper.index((r, c))] = value


def from_left(root, matrix, write):
    half = root.shape[1]
    one, two, three = root[0], root[1], root[2]
    top, bottom = matrix[:half, :], matrix[half:, :]
    write(slice(0, half), slice(None), dot(one, top) + dot(two, bottom))
    write(slice(half, 2 * half), slice(None), dot(two, top, ROWS) + dot(three, bottom))


def from_right(matrix, root, write):
    half = root.shape[1]
    one, two, three = root[0], root[1], root[2]
    before, after = matrix[:, :half], matrix[:, half:]
    write(slice(None), slice(0, half), dot(before, one) + dot(after, two, COLUMNS))
    write(slice(None), slice(half, 2 * half), dot(before, two) + dot(after, three))


def side_kernel(place, root, grad, side, grad_sum):
    core = place[0]

    def write(rows, columns, product):
        side[rows, columns] = product.astype(jnp.bfloat16)

    @pl.when(core == 0)
    def _():
        from_left(root, grad, write)

    @pl.when(core == 1)
    def _():
        from_right(grad, root, write)

    value = grad[...].astype(jnp.float32)
    grad_sum[...] = jnp.sum(value * value, axis=0, keepdims=True)


def finish_kernel(place, own, side, root, grad_sum, out, raw):
    core = place[0]
    half, width = own.shape

    def write(rows, columns, product):
        raw[rows, columns] = product

    @pl.when(core == 0)
    def _():
        from_right(side, root, write)

    @pl.when(core == 1)
    def _():
        from_left(root, side, write)

    raw_sum = jnp.sum(raw[...] * raw[...], axis=0, keepdims=True)
    scale = 1.0 / (width * width)
    grad_mean = jnp.sum(grad_sum[...], axis=1, keepdims=True) * scale
    raw_mean = jnp.sum(raw_sum, axis=1, keepdims=True) * scale
    ratio = jnp.sqrt(grad_mean + 1e-06) / jnp.sqrt(raw_mean + 1e-06)
    active = place[1] > 0

    @pl.when(active)
    def _():
        out[...] = (raw[rows_at(core * half, half), :] * ratio).astype(jnp.bfloat16)

    @pl.when(jnp.logical_not(active))
    def _():
        out[...] = own[...]


def place_kernel(targets, place, *refs):
    *pieces, out, sems = refs
    core, plane = place[0], place[2]
    copies = []
    for index, (which, skip, count, shift, start, mine) in enumerate(targets):
        rows = pieces[which].shape[1]
        half = core if mine else 1 - core
        first = lax.rem(plane + shift, 4) * (out.shape[0] // 4) + start
        copies.append(
            pltpu.make_async_copy(
                pieces[which].at[pl.ds(skip, count)],
                out.at[pl.ds(first, count), rows_at(half * rows, rows), :],
                sems.at[index],
            )
        )
    for copy in copies:
        copy.start()
    for copy in copies:
        copy.wait()


def local(partials, owned_block):
    core = lax.axis_index("core")
    plane = lax.axis_index("z")
    slot = lax.axis_index("y") * 4 + lax.axis_index("x")
    _, blocks, piece_rows, width = partials.shape
    planes = 4
    per_plane = blocks // planes
    part = per_plane // 2
    rows = piece_rows // 2
    shards = 16
    half = rows * shards
    swap = [(0, 1), (1, 0)]
    up = [(i, (i + 1) % planes) for i in range(planes)]
    down = [(i, (i - 1) % planes) for i in range(planes)]
    def plus(*terms):
        total = terms[0].astype(jnp.float32)
        for term in terms[1:]:
            total = total + term.astype(jnp.float32)
        return total.astype(jnp.bfloat16)

    smem = pl.BlockSpec(memory_space=pltpu.SMEM)
    vmem = pl.BlockSpec(memory_space=pltpu.VMEM)
    anywhere = pl.BlockSpec(memory_space=pl.ANY)
    halves = partials.reshape(planes, per_plane, 2, rows, width)

    def rows_of(here, shift, which):
        sliced = lax.dynamic_slice(
            halves, ((here + shift) % planes, 0, which, 0, 0), (1, per_plane, 1, rows, width)
        )
        return sliced.reshape(per_plane, rows, width)

    with jax.named_scope("sum_over_replicas"):
        sent, next_plane = lax.optimization_barrier((rows_of(plane, 2, 1 - core), plane))
        got = lax.ppermute(sent, "core", swap)
        kept, *sent = lax.optimization_barrier(
            [rows_of(next_plane, 2, core)] + [rows_of(next_plane, k, 1 - core) for k in (1, 3, 0)]
        )
        got_above, got_below, got_mine = (lax.ppermute(each, "core", swap) for each in sent)
        far = plus(kept, got)
        far_low, far_high, here, owners = lax.optimization_barrier(
            (far[:part], far[part:], plane, owned_block)
        )
        from_above = lax.ppermute(far_low, "z", down)
        from_below = lax.ppermute(far_high, "z", up)
        kept_above, kept_below, kept_mine = lax.optimization_barrier(
            [rows_of(here, k, core) for k in (1, 3, 0)]
        )
        to_above = plus(kept_above, got_above)
        to_below = plus(kept_below, got_below)
        mine = plus(kept_mine, got_mine)
        low_below = lax.ppermute(to_above[:part], "z", up)
        high_above = lax.ppermute(to_below[part:], "z", down)
        low_above = lax.ppermute(plus(to_below[:part], from_above), "z", down)
        high_below = lax.ppermute(plus(to_above[part:], from_below), "z", up)
        summed = jnp.concatenate(
            [
                plus(mine[:part], low_below, low_above),
                plus(mine[part:], high_above, high_below),
                jnp.zeros((shards - per_plane, rows, width), jnp.bfloat16),
            ],
            axis=0,
        )

    block = plane * per_plane + slot
    active = jnp.any(owners == block) & (slot < per_plane)
    place = jnp.stack([core, active.astype(jnp.int32), plane]).astype(jnp.int32)
    summed, place = lax.optimization_barrier((summed, place))

    with jax.named_scope("rows_to_owner"):
        own = lax.all_to_all(summed, ("y", "x"), 0, 0, tiled=True).reshape(half, width)
        sibling = lax.ppermute(own, "core", swap)

    square = (width, width)
    whole = jax.ShapeDtypeStruct(square, jnp.bfloat16)
    work = 2 * width**3
    own_root, grad = pl.pallas_call(
        root_kernel,
        out_shape=[jax.ShapeDtypeStruct((3, half, half), jnp.bfloat16), whole],
        in_specs=[smem, vmem, vmem],
        out_specs=[vmem, vmem],
        scratch_shapes=[
            pltpu.VMEM(square, jnp.float32),
            pltpu.VMEM(square, jnp.bfloat16),
            pltpu.VMEM(square, jnp.bfloat16),
            pltpu.VMEM(square, jnp.bfloat16),
        ],
        compiler_params=pltpu.CompilerParams(vmem_limit_bytes=40 * mib),
        cost_estimate=pl.CostEstimate(flops=3 * work, bytes_accessed=6 * mib, transcendentals=0),
        name="inverse_root",
    )(place, own, sibling)
    sibling_root = lax.ppermute(own_root, "core", swap)
    side, grad_sum = pl.pallas_call(
        side_kernel,
        out_shape=[whole, jax.ShapeDtypeStruct((1, width), jnp.float32)],
        in_specs=[smem, vmem, vmem],
        out_specs=[vmem, vmem],
        compiler_params=pltpu.CompilerParams(vmem_limit_bytes=32 * mib),
        cost_estimate=pl.CostEstimate(flops=work, bytes_accessed=6 * mib, transcendentals=0),
        name="apply_own_root",
    )(place, own_root, grad)
    finished = pl.pallas_call(
        finish_kernel,
        out_shape=jax.ShapeDtypeStruct((half, width), jnp.bfloat16),
        in_specs=[smem, vmem, vmem, vmem, vmem],
        out_specs=vmem,
        scratch_shapes=[pltpu.VMEM(square, jnp.float32)],
        compiler_params=pltpu.CompilerParams(vmem_limit_bytes=32 * mib),
        cost_estimate=pl.CostEstimate(flops=work, bytes_accessed=6 * mib, transcendentals=0),
        name="apply_other_root",
    )(place, own, side, sibling_root, grad_sum)

    with jax.named_scope("rows_to_shards"):
        back = lax.all_to_all(
            finished.reshape(shards, rows, width), ("y", "x"), 0, 0, tiled=True
        )[:per_plane]

    out_shape = jax.ShapeDtypeStruct((blocks, piece_rows, width), jnp.bfloat16)

    def put(name, before, *entries):
        targets, operands = [], []
        for which, (array, *runs) in enumerate(entries):
            skip = 0
            for shift, start, count, mine in runs:
                targets.append((which, skip, count, shift, start, mine))
                skip += count
            operands.append(array)
        moved = sum(4 * operand.size for operand in operands)
        operands.append(before)
        first = before.shape != out_shape.shape
        return pl.pallas_call(
            functools.partial(place_kernel, targets),
            out_shape=out_shape,
            in_specs=[smem] + [vmem] * len(entries) + [vmem if first else anywhere],
            out_specs=anywhere,
            scratch_shapes=[pltpu.SemaphoreType.DMA((len(targets),))],
            input_output_aliases={} if first else {len(operands): 0},
            compiler_params=pltpu.CompilerParams(vmem_limit_bytes=24 * mib),
            cost_estimate=pl.CostEstimate(flops=0, bytes_accessed=moved, transcendentals=0),
            name=name,
        )(place, *operands)

    def other_core(piece):
        return lax.ppermute(piece, "core", swap)

    with jax.named_scope("gather_over_replicas"):
        above_low = lax.ppermute(back[:part], "z", down)
        below_high = lax.ppermute(back[part:], "z", up)
        behind = other_core(back[:1, :16, :128])
        low, high, behind = lax.optimization_barrier((back[:part], back[part:], behind))
        above_high = lax.ppermute(high, "z", down)
        below_low = lax.ppermute(low, "z", up)
        above_low, below_high, other = lax.optimization_barrier(
            (above_low, below_high, other_core(back))
        )
        far_low = lax.ppermute(above_low, "z", down)
        far_high = lax.ppermute(below_high, "z", up)
        passed = other_core(jnp.concatenate([above_low, below_high], axis=0))
        out = put(
            "place_early",
            behind,
            (back, (0, 0, per_plane, True)),
            (other, (0, 0, per_plane, False)),
            (above_low, (1, 0, part, True)),
            (below_high, (3, part, part, True)),
        )
        above_high, below_low, out = lax.optimization_barrier((above_high, below_low, out))
        return put(
            "place_late",
            out,
            (passed, (1, 0, part, False), (3, part, part, False)),
            (above_high, (1, part, part, True)),
            (below_low, (3, 0, part, True)),
            (other_core(above_high), (1, part, part, False)),
            (other_core(below_low), (3, 0, part, False)),
            (far_low, (2, 0, part, True)),
            (far_high, (2, part, part, True)),
            (other_core(far_low), (2, 0, part, False)),
            (other_core(far_high), (2, part, part, False)),
        )


def solution(mesh):
    grid = Mesh(mesh.devices.reshape(4, 2, 4, 4), ("z", "core", "y", "x"))
    in_specs = (P(("z", "core"), None, ("y", "x"), None), P())
    out_specs = P(None, ("y", "x"), None)
    return jax.shard_map(local, mesh=grid, in_specs=in_specs, out_specs=out_specs, check_vma=False)
```

```python
import functools

import jax
import jax.numpy as jnp
from jax import lax
from jax.experimental import pallas as pl
from jax.experimental.pallas import tpu as pltpu
from jax.sharding import Mesh, PartitionSpec as P

damping = 0.1
mib = 2**20
TILE = 256
ROWS = ((0,), (0,))
COLUMNS = ((1,), (1,))


def dot(a, b, contract=((1,), (0,))):
    return lax.dot_general(a, b, (contract, ((), ())), preferred_element_type=jnp.float32)


def rows_at(start, count):
    return pl.ds(pl.multiple_of(start, count), count)


def root_kernel(place, own, sibling, root, grad, stat, step, square, coupled, fourth):
    core = place[0]
    half, width = own.shape
    grad[rows_at(core * half, half), :] = own[...]
    grad[rows_at((1 - core) * half, half), :] = sibling[...]
    count = width // TILE
    tiles = [slice(i * TILE, (i + 1) * TILE) for i in range(count)]
    tails = [slice(i * TILE, width) for i in range(count)]
    eye = lax.broadcasted_iota(jnp.int32, (TILE, TILE), 0) == lax.broadcasted_iota(
        jnp.int32, (TILE, TILE), 1
    )

    def squares(value):
        return jnp.sum(value * value, axis=0, keepdims=True)

    def add_up(value):
        return jnp.sum(value, axis=1, keepdims=True)

    def statistic(contract):
        total = jnp.zeros((1, 1), jnp.float32)
        for i in range(count):
            if contract == ROWS:
                product = dot(grad[:, tiles[i]], grad[:, tails[i]], ROWS)
            else:
                product = dot(grad[tiles[i], :], grad[tails[i], :], COLUMNS)
            value = product * (1.0 / width)
            block = value[:, :TILE] + jnp.where(eye, damping, 0.0)
            stat[tiles[i], tiles[i]] = block
            total = total + add_up(squares(block))
            if i + 1 < count:
                stat[tiles[i], tails[i + 1]] = value[:, TILE:]
                total = total + 2.0 * add_up(squares(value[:, TILE:]))
        return total

    total = lax.cond(core == 0, lambda: statistic(COLUMNS), lambda: statistic(ROWS))
    inverse = 4.0 * lax.rsqrt(total)

    def rest(matrix, i):
        if i + 1 < count:
            matrix[tails[i + 1], tiles[i]] = matrix[tiles[i], tails[i + 1]].T

    across, along = [], []
    for i in range(count):
        matrix = (stat[tiles[i], tails[i]] * inverse).astype(jnp.bfloat16).astype(jnp.float32)
        block = matrix[:, :TILE]
        value = ((jnp.where(eye, 5.0, 0.0) - block) * 0.25).astype(jnp.bfloat16)
        both = jnp.where(eye, 4.0 * value.astype(jnp.float32) + block, 0.0)
        across.append(jnp.sum(both, axis=0, keepdims=True))
        along.append(jnp.sum(both, axis=1, keepdims=True))
        step[tiles[i], tiles[i]] = value
        if i + 1 < count:
            step[tiles[i], tails[i + 1]] = (matrix[:, TILE:] * -0.25).astype(jnp.bfloat16)
            rest(step, i)
    across = jnp.concatenate(across, axis=1)
    for i in range(count):
        product = dot(step[tiles[i], :], step[:, tails[i]])
        square[tiles[i], tails[i]] = product.astype(jnp.bfloat16)
        rest(square, i)
        value = step[tiles[i], tails[i]].astype(jnp.float32)
        coupled[tiles[i], tails[i]] = (value * across[:, tails[i]] - 4.0 * product).astype(
            jnp.bfloat16
        )
        if i + 1 < count:
            below = value[:, TILE:] * along[i] - 4.0 * product[:, TILE:]
            coupled[tails[i + 1], tiles[i]] = below.astype(jnp.bfloat16).T
    for i in range(count):
        product = dot(square[tiles[i], :], square[:, tails[i]])
        fourth[tiles[i], tails[i]] = product.astype(jnp.bfloat16)
        rest(fourth, i)
    for i in range(count):
        product = dot(fourth[tiles[i], :], coupled[:, tails[i]])
        value = step[tiles[i], tails[i]].astype(jnp.float32)
        value = ((5.0 * value - product) * 0.25).astype(jnp.bfloat16)
        start = i * TILE
        if start < half:
            root[0, tiles[i], start:half] = value[:, : half - start]
            root[1, tiles[i], :] = value[:, half - start :]
            if start + TILE < half:
                root[0, start + TILE : half, tiles[i]] = value[:, TILE : half - start].T
        else:
            rows, columns = slice(start - half, start - half + TILE), slice(start - half, half)
            root[2, rows, columns] = value
            if start + TILE < width:
                root[2, start - half + TILE : half, rows] = value[:, TILE:].T


def from_left(root, matrix, write):
    half = root.shape[1]
    one, two, three = root[0], root[1], root[2]
    top, bottom = matrix[:half, :], matrix[half:, :]
    write(slice(0, half), slice(None), dot(one, top) + dot(two, bottom))
    write(slice(half, 2 * half), slice(None), dot(two, top, ROWS) + dot(three, bottom))


def from_right(matrix, root, write):
    half = root.shape[1]
    one, two, three = root[0], root[1], root[2]
    before, after = matrix[:, :half], matrix[:, half:]
    write(slice(None), slice(0, half), dot(before, one) + dot(after, two, COLUMNS))
    write(slice(None), slice(half, 2 * half), dot(before, two) + dot(after, three))


def side_kernel(place, root, grad, side, grad_sum):
    core = place[0]

    def write(rows, columns, product):
        side[rows, columns] = product.astype(jnp.bfloat16)

    @pl.when(core == 0)
    def _():
        from_left(root, grad, write)

    @pl.when(core == 1)
    def _():
        from_right(grad, root, write)

    value = grad[...].astype(jnp.float32)
    grad_sum[...] = jnp.sum(value * value, axis=0, keepdims=True)


def finish_kernel(place, own, side, root, grad_sum, out, raw):
    core = place[0]
    half, width = own.shape

    def write(rows, columns, product):
        raw[rows, columns] = product
        square = jnp.sum(product * product, axis=0, keepdims=True)
        sums.append(jnp.sum(square, axis=1, keepdims=True))

    def left():
        sums.clear()
        from_left(root, side, write)
        return sums[0] + sums[1]

    def right():
        sums.clear()
        from_right(side, root, write)
        return sums[0] + sums[1]

    sums = []
    raw_sum = lax.cond(core == 0, right, left)
    scale = 1.0 / (width * width)
    grad_mean = jnp.sum(grad_sum[...], axis=1, keepdims=True) * scale
    raw_mean = jnp.sum(raw_sum, axis=1, keepdims=True) * scale
    ratio = jnp.sqrt(grad_mean + 1e-06) / jnp.sqrt(raw_mean + 1e-06)
    active = place[1] > 0

    @pl.when(active)
    def _():
        out[...] = (raw[rows_at(core * half, half), :] * ratio).astype(jnp.bfloat16)

    @pl.when(jnp.logical_not(active))
    def _():
        out[...] = own[...]


def place_kernel(targets, place, *refs):
    *pieces, out, sems = refs
    core, plane = place[0], place[2]
    copies = []
    for index, (which, skip, count, shift, start, mine) in enumerate(targets):
        rows = pieces[which].shape[1]
        half = core if mine else 1 - core
        first = lax.rem(plane + shift, 4) * (out.shape[0] // 4) + start
        copies.append(
            pltpu.make_async_copy(
                pieces[which].at[pl.ds(skip, count)],
                out.at[pl.ds(first, count), rows_at(half * rows, rows), :],
                sems.at[index],
            )
        )
    for copy in copies:
        copy.start()
    for copy in copies:
        copy.wait()


def local(partials, owned_block):
    core = lax.axis_index("core")
    plane = lax.axis_index("z")
    slot = lax.axis_index("y") * 4 + lax.axis_index("x")
    _, blocks, piece_rows, width = partials.shape
    planes = 4
    per_plane = blocks // planes
    part = per_plane // 2
    rows = piece_rows // 2
    shards = 16
    half = rows * shards
    swap = [(0, 1), (1, 0)]
    up = [(i, (i + 1) % planes) for i in range(planes)]
    down = [(i, (i - 1) % planes) for i in range(planes)]
    def plus(*terms):
        total = terms[0].astype(jnp.float32)
        for term in terms[1:]:
            total = total + term.astype(jnp.float32)
        return total.astype(jnp.bfloat16)

    smem = pl.BlockSpec(memory_space=pltpu.SMEM)
    vmem = pl.BlockSpec(memory_space=pltpu.VMEM)
    anywhere = pl.BlockSpec(memory_space=pl.ANY)
    halves = partials.reshape(planes, per_plane, 2, rows, width)

    def rows_of(here, shift, which):
        sliced = lax.dynamic_slice(
            halves, ((here + shift) % planes, 0, which, 0, 0), (1, per_plane, 1, rows, width)
        )
        return sliced.reshape(per_plane, rows, width)

    with jax.named_scope("sum_over_replicas"):
        sent, next_plane = lax.optimization_barrier((rows_of(plane, 2, 1 - core), plane))
        got = lax.ppermute(sent, "core", swap)
        kept, *sent = lax.optimization_barrier(
            [rows_of(next_plane, 2, core)] + [rows_of(next_plane, k, 1 - core) for k in (1, 3, 0)]
        )
        got_above, got_below, got_mine = (lax.ppermute(each, "core", swap) for each in sent)
        far = plus(kept, got)
        far_low, far_high, here = lax.optimization_barrier((far[:part], far[part:], plane))
        from_above = lax.ppermute(far_low, "z", down)
        from_below = lax.ppermute(far_high, "z", up)
        kept_above, kept_below, kept_mine = lax.optimization_barrier(
            [rows_of(here, k, core) for k in (1, 3, 0)]
        )
        to_above = plus(kept_above, got_above)
        to_below = plus(kept_below, got_below)
        mine = plus(kept_mine, got_mine)
        low_below = lax.ppermute(to_above[:part], "z", up)
        high_above = lax.ppermute(to_below[part:], "z", down)
        low_below, owners = lax.optimization_barrier((low_below, owned_block))
        low_above = lax.ppermute(plus(to_below[:part], from_above), "z", down)
        high_below = lax.ppermute(plus(to_above[part:], from_below), "z", up)
        summed = jnp.concatenate(
            [
                plus(mine[:part], low_below, low_above),
                plus(mine[part:], high_above, high_below),
                jnp.zeros((shards - per_plane, rows, width), jnp.bfloat16),
            ],
            axis=0,
        )

    block = plane * per_plane + slot
    active = jnp.any(owners == block) & (slot < per_plane)
    place = jnp.stack([core, active.astype(jnp.int32), plane]).astype(jnp.int32)
    summed, place = lax.optimization_barrier((summed, place))

    with jax.named_scope("rows_to_owner"):
        own = lax.all_to_all(summed, ("y", "x"), 0, 0, tiled=True).reshape(half, width)
        sibling = lax.ppermute(own, "core", swap)

    square = (width, width)
    whole = jax.ShapeDtypeStruct(square, jnp.bfloat16)
    work = 2 * width**3
    own_root, grad = pl.pallas_call(
        root_kernel,
        out_shape=[jax.ShapeDtypeStruct((3, half, half), jnp.bfloat16), whole],
        in_specs=[smem, vmem, vmem],
        out_specs=[vmem, vmem],
        scratch_shapes=[
            pltpu.VMEM(square, jnp.float32),
        ]
        + [pltpu.VMEM(square, jnp.bfloat16)] * 4,
        compiler_params=pltpu.CompilerParams(vmem_limit_bytes=40 * mib),
        cost_estimate=pl.CostEstimate(flops=3 * work, bytes_accessed=6 * mib, transcendentals=0),
        name="inverse_root",
    )(place, own, sibling)
    sibling_root = lax.ppermute(own_root, "core", swap)
    side, grad_sum = pl.pallas_call(
        side_kernel,
        out_shape=[whole, jax.ShapeDtypeStruct((1, width), jnp.float32)],
        in_specs=[smem, vmem, vmem],
        out_specs=[vmem, vmem],
        compiler_params=pltpu.CompilerParams(vmem_limit_bytes=32 * mib),
        cost_estimate=pl.CostEstimate(flops=work, bytes_accessed=6 * mib, transcendentals=0),
        name="apply_own_root",
    )(place, own_root, grad)
    finished = pl.pallas_call(
        finish_kernel,
        out_shape=jax.ShapeDtypeStruct((half, width), jnp.bfloat16),
        in_specs=[smem, vmem, vmem, vmem, vmem],
        out_specs=vmem,
        scratch_shapes=[pltpu.VMEM(square, jnp.float32)],
        compiler_params=pltpu.CompilerParams(vmem_limit_bytes=32 * mib),
        cost_estimate=pl.CostEstimate(flops=work, bytes_accessed=6 * mib, transcendentals=0),
        name="apply_other_root",
    )(place, own, side, sibling_root, grad_sum)

    with jax.named_scope("rows_to_shards"):
        back = lax.all_to_all(
            finished.reshape(shards, rows, width), ("y", "x"), 0, 0, tiled=True
        )[:per_plane]

    out_shape = jax.ShapeDtypeStruct((blocks, piece_rows, width), jnp.bfloat16)

    def put(name, before, *entries):
        targets, operands = [], []
        for which, (array, *runs) in enumerate(entries):
            skip = 0
            for shift, start, count, mine in runs:
                targets.append((which, skip, count, shift, start, mine))
                skip += count
            operands.append(array)
        moved = sum(4 * operand.size for operand in operands)
        operands.append(before)
        first = before.shape != out_shape.shape
        return pl.pallas_call(
            functools.partial(place_kernel, targets),
            out_shape=out_shape,
            in_specs=[smem] + [vmem] * len(entries) + [vmem if first else anywhere],
            out_specs=anywhere,
            scratch_shapes=[pltpu.SemaphoreType.DMA((len(targets),))],
            input_output_aliases={} if first else {len(operands): 0},
            compiler_params=pltpu.CompilerParams(vmem_limit_bytes=24 * mib),
            cost_estimate=pl.CostEstimate(flops=0, bytes_accessed=moved, transcendentals=0),
            name=name,
        )(place, *operands)

    def other_core(piece):
        return lax.ppermute(piece, "core", swap)

    with jax.named_scope("gather_over_replicas"):
        above_low = lax.ppermute(back[:part], "z", down)
        below_high = lax.ppermute(back[part:], "z", up)
        behind = other_core(back[:1, :16, :128])
        low, high, behind = lax.optimization_barrier((back[:part], back[part:], behind))
        above_high = lax.ppermute(high, "z", down)
        below_low = lax.ppermute(low, "z", up)
        above_low, below_high, other = lax.optimization_barrier(
            (above_low, below_high, other_core(back))
        )
        far_low = lax.ppermute(above_low, "z", down)
        far_high = lax.ppermute(below_high, "z", up)
        passed = other_core(jnp.concatenate([above_low, below_high], axis=0))
        out = put(
            "place_early",
            behind,
            (back, (0, 0, per_plane, True)),
            (other, (0, 0, per_plane, False)),
            (above_low, (1, 0, part, True)),
            (below_high, (3, part, part, True)),
        )
        above_high, below_low, out = lax.optimization_barrier((above_high, below_low, out))
        return put(
            "place_late",
            out,
            (passed, (1, 0, part, False), (3, part, part, False)),
            (above_high, (1, part, part, True)),
            (below_low, (3, 0, part, True)),
            (other_core(above_high), (1, part, part, False)),
            (other_core(below_low), (3, 0, part, False)),
            (far_low, (2, 0, part, True)),
            (far_high, (2, part, part, True)),
            (other_core(far_low), (2, 0, part, False)),
            (other_core(far_high), (2, part, part, False)),
        )


def solution(mesh):
    grid = Mesh(mesh.devices.reshape(4, 2, 4, 4), ("z", "core", "y", "x"))
    in_specs = (P(("z", "core"), None, ("y", "x"), None), P())
    out_specs = P(None, ("y", "x"), None)
    return jax.shard_map(local, mesh=grid, in_specs=in_specs, out_specs=out_specs, check_vma=False)
```

```python
import functools

import jax
import jax.numpy as jnp
from jax import lax
from jax.experimental import pallas as pl
from jax.experimental.pallas import tpu as pltpu
from jax.sharding import Mesh, PartitionSpec as P

damping = 0.1
mib = 2**20
TILE = 256
ROWS = ((0,), (0,))
COLUMNS = ((1,), (1,))


def dot(a, b, contract=((1,), (0,))):
    return lax.dot_general(a, b, (contract, ((), ())), preferred_element_type=jnp.float32)


def rows_at(start, count):
    return pl.ds(pl.multiple_of(start, count), count)


def root_kernel(place, own, sibling, root, grad, stat, step, square, coupled, fourth):
    core = place[0]
    half, width = own.shape
    grad[rows_at(core * half, half), :] = own[...]
    grad[rows_at((1 - core) * half, half), :] = sibling[...]
    count = width // TILE
    tiles = [slice(i * TILE, (i + 1) * TILE) for i in range(count)]
    tails = [slice(i * TILE, width) for i in range(count)]
    eye = lax.broadcasted_iota(jnp.int32, (TILE, TILE), 0) == lax.broadcasted_iota(
        jnp.int32, (TILE, TILE), 1
    )

    def squares(value):
        return jnp.sum(value * value, axis=0, keepdims=True)

    def add_up(value):
        return jnp.sum(value, axis=1, keepdims=True)

    def statistic(contract):
        total = jnp.zeros((1, 1), jnp.float32)
        for i in range(count):
            if contract == ROWS:
                product = dot(grad[:, tiles[i]], grad[:, tails[i]], ROWS)
            else:
                product = dot(grad[tiles[i], :], grad[tails[i], :], COLUMNS)
            value = product * (1.0 / width)
            block = value[:, :TILE] + jnp.where(eye, damping, 0.0)
            stat[tiles[i], tiles[i]] = block
            total = total + add_up(squares(block))
            if i + 1 < count:
                stat[tiles[i], tails[i + 1]] = value[:, TILE:]
                total = total + 2.0 * add_up(squares(value[:, TILE:]))
        return total

    total = lax.cond(core == 0, lambda: statistic(COLUMNS), lambda: statistic(ROWS))
    inverse = 4.0 * lax.rsqrt(total)

    def rest(matrix, i):
        if i + 1 < count:
            matrix[tails[i + 1], tiles[i]] = matrix[tiles[i], tails[i + 1]].T

    across, along = [], []
    for i in range(count):
        matrix = (stat[tiles[i], tails[i]] * inverse).astype(jnp.bfloat16).astype(jnp.float32)
        block = matrix[:, :TILE]
        value = ((jnp.where(eye, 5.0, 0.0) - block) * 0.25).astype(jnp.bfloat16)
        both = jnp.where(eye, 4.0 * value.astype(jnp.float32) + block, 0.0)
        across.append(jnp.sum(both, axis=0, keepdims=True))
        along.append(jnp.sum(both, axis=1, keepdims=True))
        step[tiles[i], tiles[i]] = value
        if i + 1 < count:
            step[tiles[i], tails[i + 1]] = (matrix[:, TILE:] * -0.25).astype(jnp.bfloat16)
            rest(step, i)
    across = jnp.concatenate(across, axis=1)
    for i in range(count):
        product = dot(step[tiles[i], :], step[:, tails[i]])
        square[tiles[i], tails[i]] = product.astype(jnp.bfloat16)
        rest(square, i)
        value = step[tiles[i], tails[i]].astype(jnp.float32)
        coupled[tiles[i], tails[i]] = (value * across[:, tails[i]] - 4.0 * product).astype(
            jnp.bfloat16
        )
        if i + 1 < count:
            below = value[:, TILE:] * along[i] - 4.0 * product[:, TILE:]
            coupled[tails[i + 1], tiles[i]] = below.astype(jnp.bfloat16).T
    for i in range(count):
        product = dot(square[tiles[i], :], square[:, tails[i]])
        fourth[tiles[i], tails[i]] = product.astype(jnp.bfloat16)
        rest(fourth, i)
    for i in range(count):
        product = dot(fourth[tiles[i], :], coupled[:, tails[i]])
        value = step[tiles[i], tails[i]].astype(jnp.float32)
        value = ((5.0 * value - product) * 0.25).astype(jnp.bfloat16)
        start = i * TILE
        if start < half:
            root[0, tiles[i], start:half] = value[:, : half - start]
            root[1, tiles[i], :] = value[:, half - start :]
            if start + TILE < half:
                root[0, start + TILE : half, tiles[i]] = value[:, TILE : half - start].T
        else:
            rows, columns = slice(start - half, start - half + TILE), slice(start - half, half)
            root[2, rows, columns] = value
            if start + TILE < width:
                root[2, start - half + TILE : half, rows] = value[:, TILE:].T


def from_left(root, matrix, write):
    half = root.shape[1]
    one, two, three = root[0], root[1], root[2]
    top, bottom = matrix[:half, :], matrix[half:, :]
    write(slice(0, half), slice(None), dot(one, top) + dot(two, bottom))
    write(slice(half, 2 * half), slice(None), dot(two, top, ROWS) + dot(three, bottom))


def from_right(matrix, root, write):
    half = root.shape[1]
    one, two, three = root[0], root[1], root[2]
    before, after = matrix[:, :half], matrix[:, half:]
    write(slice(None), slice(0, half), dot(before, one) + dot(after, two, COLUMNS))
    write(slice(None), slice(half, 2 * half), dot(before, two) + dot(after, three))


def side_kernel(place, root, grad, side, grad_sum):
    core = place[0]

    def write(rows, columns, product):
        side[rows, columns] = product.astype(jnp.bfloat16)

    @pl.when(core == 0)
    def _():
        from_left(root, grad, write)

    @pl.when(core == 1)
    def _():
        from_right(grad, root, write)

    value = grad[...].astype(jnp.float32)
    grad_sum[...] = jnp.sum(value * value, axis=0, keepdims=True)


def finish_kernel(place, own, side, root, grad_sum, out, raw):
    core = place[0]
    half, width = own.shape

    sums = []

    def add_up(product):
        squares = jnp.sum(product * product, axis=0, keepdims=True)
        sums.append(jnp.sum(squares, axis=1, keepdims=True))

    def write_first(rows, columns, product):
        raw[:, columns] = product[:half]
        add_up(product)

    def write_last(rows, columns, product):
        if rows.start == half:
            raw[...] = product
        add_up(product)

    def right():
        sums.clear()
        from_right(side, root, write_first)
        return sums[0] + sums[1]

    def left():
        sums.clear()
        from_left(root, side, write_last)
        return sums[0] + sums[1]

    raw_sum = lax.cond(core == 0, right, left)
    scale = 1.0 / (width * width)
    grad_mean = jnp.sum(grad_sum[...], axis=1, keepdims=True) * scale
    raw_mean = jnp.sum(raw_sum, axis=1, keepdims=True) * scale
    ratio = jnp.sqrt(grad_mean + 1e-06) / jnp.sqrt(raw_mean + 1e-06)
    active = place[1] > 0

    @pl.when(active)
    def _():
        out[...] = (raw[...] * ratio).astype(jnp.bfloat16)

    @pl.when(jnp.logical_not(active))
    def _():
        out[...] = own[...]


def place_kernel(targets, place, *refs):
    *pieces, out, sems = refs
    core, plane = place[0], place[2]
    copies = []
    for index, (which, skip, count, shift, start, mine) in enumerate(targets):
        rows = pieces[which].shape[1]
        half = core if mine else 1 - core
        first = lax.rem(plane + shift, 4) * (out.shape[0] // 4) + start
        copies.append(
            pltpu.make_async_copy(
                pieces[which].at[pl.ds(skip, count)],
                out.at[pl.ds(first, count), rows_at(half * rows, rows), :],
                sems.at[index],
            )
        )
    for copy in copies:
        copy.start()
    for copy in copies:
        copy.wait()


def local(partials, owned_block):
    core = lax.axis_index("core")
    plane = lax.axis_index("z")
    slot = lax.axis_index("y") * 4 + lax.axis_index("x")
    _, blocks, piece_rows, width = partials.shape
    planes = 4
    per_plane = blocks // planes
    part = per_plane // 2
    rows = piece_rows // 2
    shards = 16
    half = rows * shards
    swap = [(0, 1), (1, 0)]
    up = [(i, (i + 1) % planes) for i in range(planes)]
    down = [(i, (i - 1) % planes) for i in range(planes)]
    def plus(*terms):
        total = terms[0].astype(jnp.float32)
        for term in terms[1:]:
            total = total + term.astype(jnp.float32)
        return total.astype(jnp.bfloat16)

    smem = pl.BlockSpec(memory_space=pltpu.SMEM)
    vmem = pl.BlockSpec(memory_space=pltpu.VMEM)
    anywhere = pl.BlockSpec(memory_space=pl.ANY)
    halves = partials.reshape(planes, per_plane, 2, rows, width)

    def rows_of(here, shift, which):
        sliced = lax.dynamic_slice(
            halves, ((here + shift) % planes, 0, which, 0, 0), (1, per_plane, 1, rows, width)
        )
        return sliced.reshape(per_plane, rows, width)

    with jax.named_scope("sum_over_replicas"):
        sent, kept, *others = lax.optimization_barrier(
            [rows_of(plane, 2, 1 - core), rows_of(plane, 2, core)]
            + [rows_of(plane, k, 1 - core) for k in (1, 3, 0)]
        )
        got = lax.ppermute(sent, "core", swap)
        got_above, got_below, got_mine = (lax.ppermute(each, "core", swap) for each in others)
        far = plus(kept, got)
        far_low, far_high, here = lax.optimization_barrier((far[:part], far[part:], plane))
        from_above = lax.ppermute(far_low, "z", down)
        from_below = lax.ppermute(far_high, "z", up)
        kept_above, kept_below, kept_mine = lax.optimization_barrier(
            [rows_of(here, k, core) for k in (1, 3, 0)]
        )
        to_above = plus(kept_above, got_above)
        to_below = plus(kept_below, got_below)
        mine = plus(kept_mine, got_mine)
        low_below = lax.ppermute(to_above[:part], "z", up)
        high_above = lax.ppermute(to_below[part:], "z", down)
        low_below, owners = lax.optimization_barrier((low_below, owned_block))
        low_above = lax.ppermute(plus(to_below[:part], from_above), "z", down)
        high_below = lax.ppermute(plus(to_above[part:], from_below), "z", up)
        summed = jnp.concatenate(
            [
                plus(mine[:part], low_below, low_above),
                plus(mine[part:], high_above, high_below),
                jnp.zeros((shards - per_plane, rows, width), jnp.bfloat16),
            ],
            axis=0,
        )

    block = plane * per_plane + slot
    active = jnp.any(owners == block) & (slot < per_plane)
    place = jnp.stack([core, active.astype(jnp.int32), plane]).astype(jnp.int32)
    summed, place = lax.optimization_barrier((summed, place))

    with jax.named_scope("rows_to_owner"):
        own = lax.all_to_all(summed, ("y", "x"), 0, 0, tiled=True).reshape(half, width)
        sibling = lax.ppermute(own, "core", swap)

    square = (width, width)
    whole = jax.ShapeDtypeStruct(square, jnp.bfloat16)
    work = 2 * width**3
    own_root, grad = pl.pallas_call(
        root_kernel,
        out_shape=[jax.ShapeDtypeStruct((3, half, half), jnp.bfloat16), whole],
        in_specs=[smem, vmem, vmem],
        out_specs=[vmem, vmem],
        scratch_shapes=[
            pltpu.VMEM(square, jnp.float32),
        ]
        + [pltpu.VMEM(square, jnp.bfloat16)] * 4,
        compiler_params=pltpu.CompilerParams(vmem_limit_bytes=40 * mib),
        cost_estimate=pl.CostEstimate(flops=3 * work, bytes_accessed=6 * mib, transcendentals=0),
        name="inverse_root",
    )(place, own, sibling)
    sibling_root = lax.ppermute(own_root, "core", swap)
    side, grad_sum = pl.pallas_call(
        side_kernel,
        out_shape=[whole, jax.ShapeDtypeStruct((1, width), jnp.float32)],
        in_specs=[smem, vmem, vmem],
        out_specs=[vmem, vmem],
        compiler_params=pltpu.CompilerParams(vmem_limit_bytes=32 * mib),
        cost_estimate=pl.CostEstimate(flops=work, bytes_accessed=6 * mib, transcendentals=0),
        name="apply_own_root",
    )(place, own_root, grad)
    finished = pl.pallas_call(
        finish_kernel,
        out_shape=jax.ShapeDtypeStruct((half, width), jnp.bfloat16),
        in_specs=[smem, vmem, vmem, vmem, vmem],
        out_specs=vmem,
        scratch_shapes=[pltpu.VMEM((half, width), jnp.float32)],
        compiler_params=pltpu.CompilerParams(vmem_limit_bytes=32 * mib),
        cost_estimate=pl.CostEstimate(flops=work, bytes_accessed=6 * mib, transcendentals=0),
        name="apply_other_root",
    )(place, own, side, sibling_root, grad_sum)

    with jax.named_scope("rows_to_shards"):
        back = lax.all_to_all(
            finished.reshape(shards, rows, width), ("y", "x"), 0, 0, tiled=True
        )[:per_plane]

    out_shape = jax.ShapeDtypeStruct((blocks, piece_rows, width), jnp.bfloat16)

    def put(name, before, *entries):
        targets, operands = [], []
        for which, (array, *runs) in enumerate(entries):
            skip = 0
            for shift, start, count, mine in runs:
                targets.append((which, skip, count, shift, start, mine))
                skip += count
            operands.append(array)
        moved = sum(4 * operand.size for operand in operands)
        operands.append(before)
        first = before.shape != out_shape.shape
        return pl.pallas_call(
            functools.partial(place_kernel, targets),
            out_shape=out_shape,
            in_specs=[smem] + [vmem] * len(entries) + [vmem if first else anywhere],
            out_specs=anywhere,
            scratch_shapes=[pltpu.SemaphoreType.DMA((len(targets),))],
            input_output_aliases={} if first else {len(operands): 0},
            compiler_params=pltpu.CompilerParams(vmem_limit_bytes=24 * mib),
            cost_estimate=pl.CostEstimate(flops=0, bytes_accessed=moved, transcendentals=0),
            name=name,
        )(place, *operands)

    def other_core(piece):
        return lax.ppermute(piece, "core", swap)

    with jax.named_scope("gather_over_replicas"):
        above_low = lax.ppermute(back[:part], "z", down)
        below_high = lax.ppermute(back[part:], "z", up)
        behind = other_core(back[:1, :16, :128])
        low, high, behind = lax.optimization_barrier((back[:part], back[part:], behind))
        above_high = lax.ppermute(high, "z", down)
        below_low = lax.ppermute(low, "z", up)
        above_low, below_high, other = lax.optimization_barrier(
            (above_low, below_high, other_core(back))
        )
        far_low = lax.ppermute(above_low, "z", down)
        far_high = lax.ppermute(below_high, "z", up)
        passed = other_core(jnp.concatenate([above_low, below_high], axis=0))
        out = put(
            "place_early",
            behind,
            (back, (0, 0, per_plane, True)),
            (other, (0, 0, per_plane, False)),
            (above_low, (1, 0, part, True)),
            (below_high, (3, part, part, True)),
        )
        above_high, below_low, out = lax.optimization_barrier((above_high, below_low, out))
        return put(
            "place_late",
            out,
            (passed, (1, 0, part, False), (3, part, part, False)),
            (above_high, (1, part, part, True)),
            (below_low, (3, 0, part, True)),
            (other_core(above_high), (1, part, part, False)),
            (other_core(below_low), (3, 0, part, False)),
            (far_low, (2, 0, part, True)),
            (far_high, (2, part, part, True)),
            (other_core(far_low), (2, 0, part, False)),
            (other_core(far_high), (2, part, part, False)),
        )


def solution(mesh):
    grid = Mesh(mesh.devices.reshape(4, 2, 4, 4), ("z", "core", "y", "x"))
    in_specs = (P(("z", "core"), None, ("y", "x"), None), P())
    out_specs = P(None, ("y", "x"), None)
    return jax.shard_map(local, mesh=grid, in_specs=in_specs, out_specs=out_specs, check_vma=False)
```

```python
import functools

import jax
import jax.numpy as jnp
from jax import lax
from jax.experimental import pallas as pl
from jax.experimental.pallas import tpu as pltpu
from jax.sharding import Mesh, PartitionSpec as P

damping = 0.1
mib = 2**20
TILE = 256
ROWS = ((0,), (0,))
COLUMNS = ((1,), (1,))


def dot(a, b, contract=((1,), (0,))):
    return lax.dot_general(a, b, (contract, ((), ())), preferred_element_type=jnp.float32)


def rows_at(start, count):
    return pl.ds(pl.multiple_of(start, count), count)


def root_kernel(place, own, sibling, root, grad, stat, step, square, coupled, fourth):
    core = place[0]
    half, width = own.shape
    grad[rows_at(core * half, half), :] = own[...]
    grad[rows_at((1 - core) * half, half), :] = sibling[...]
    count = width // TILE
    tiles = [slice(i * TILE, (i + 1) * TILE) for i in range(count)]
    tails = [slice(i * TILE, width) for i in range(count)]
    eye = lax.broadcasted_iota(jnp.int32, (TILE, TILE), 0) == lax.broadcasted_iota(
        jnp.int32, (TILE, TILE), 1
    )

    def squares(value):
        return jnp.sum(value * value, axis=0, keepdims=True)

    def add_up(value):
        return jnp.sum(value, axis=1, keepdims=True)

    def statistic(contract):
        total = jnp.zeros((1, 1), jnp.float32)
        for i in range(count):
            if contract == ROWS:
                product = dot(grad[:, tiles[i]], grad[:, tails[i]], ROWS)
            else:
                product = dot(grad[tiles[i], :], grad[tails[i], :], COLUMNS)
            value = product * (1.0 / width)
            block = value[:, :TILE] + jnp.where(eye, damping, 0.0)
            stat[tiles[i], tiles[i]] = block
            total = total + add_up(squares(block))
            if i + 1 < count:
                stat[tiles[i], tails[i + 1]] = value[:, TILE:]
                total = total + 2.0 * add_up(squares(value[:, TILE:]))
        return total

    total = lax.cond(core == 0, lambda: statistic(COLUMNS), lambda: statistic(ROWS))
    inverse = 4.0 * lax.rsqrt(total)

    def rest(matrix, i):
        if i + 1 < count:
            matrix[tails[i + 1], tiles[i]] = matrix[tiles[i], tails[i + 1]].T

    across, along = [], []
    for i in range(count):
        matrix = (stat[tiles[i], tails[i]] * inverse).astype(jnp.bfloat16).astype(jnp.float32)
        block = matrix[:, :TILE]
        value = ((jnp.where(eye, 5.0, 0.0) - block) * 0.25).astype(jnp.bfloat16)
        both = jnp.where(eye, 4.0 * value.astype(jnp.float32) + block, 0.0)
        across.append(jnp.sum(both, axis=0, keepdims=True))
        along.append(jnp.sum(both, axis=1, keepdims=True))
        step[tiles[i], tiles[i]] = value
        if i + 1 < count:
            step[tiles[i], tails[i + 1]] = (matrix[:, TILE:] * -0.25).astype(jnp.bfloat16)
            rest(step, i)
    across = jnp.concatenate(across, axis=1)
    for i in range(count):
        product = dot(step[tiles[i], :], step[:, tails[i]])
        square[tiles[i], tails[i]] = product.astype(jnp.bfloat16)
        rest(square, i)
        value = step[tiles[i], tails[i]].astype(jnp.float32)
        coupled[tiles[i], tails[i]] = (value * across[:, tails[i]] - 4.0 * product).astype(
            jnp.bfloat16
        )
        if i + 1 < count:
            below = value[:, TILE:] * along[i] - 4.0 * product[:, TILE:]
            coupled[tails[i + 1], tiles[i]] = below.astype(jnp.bfloat16).T
    for i in range(count):
        product = dot(square[tiles[i], :], square[:, tails[i]])
        fourth[tiles[i], tails[i]] = product.astype(jnp.bfloat16)
        rest(fourth, i)
    for i in range(count):
        product = dot(fourth[tiles[i], :], coupled[:, tails[i]])
        value = step[tiles[i], tails[i]].astype(jnp.float32)
        value = ((5.0 * value - product) * 0.25).astype(jnp.bfloat16)
        start = i * TILE
        if start < half:
            root[0, tiles[i], start:half] = value[:, : half - start]
            root[1, tiles[i], :] = value[:, half - start :]
            if start + TILE < half:
                root[0, start + TILE : half, tiles[i]] = value[:, TILE : half - start].T
        else:
            rows, columns = slice(start - half, start - half + TILE), slice(start - half, half)
            root[2, rows, columns] = value
            if start + TILE < width:
                root[2, start - half + TILE : half, rows] = value[:, TILE:].T


def from_left(root, matrix, write):
    half = root.shape[1]
    one, two, three = root[0], root[1], root[2]
    top, bottom = matrix[:half, :], matrix[half:, :]
    write(slice(0, half), slice(None), dot(one, top) + dot(two, bottom))
    write(slice(half, 2 * half), slice(None), dot(two, top, ROWS) + dot(three, bottom))


def from_right(matrix, root, write):
    half = root.shape[1]
    one, two, three = root[0], root[1], root[2]
    before, after = matrix[:, :half], matrix[:, half:]
    write(slice(None), slice(0, half), dot(before, one) + dot(after, two, COLUMNS))
    write(slice(None), slice(half, 2 * half), dot(before, two) + dot(after, three))


def side_kernel(place, root, grad, side, grad_sum):
    core = place[0]

    def write(rows, columns, product):
        side[rows, columns] = product.astype(jnp.bfloat16)

    @pl.when(core == 0)
    def _():
        from_left(root, grad, write)

    @pl.when(core == 1)
    def _():
        from_right(grad, root, write)

    value = grad[...].astype(jnp.float32)
    grad_sum[...] = jnp.sum(value * value, axis=0, keepdims=True)


def finish_kernel(place, own, side, root, grad_sum, out, raw):
    core = place[0]
    half, width = own.shape

    def write(rows, columns, product):
        raw[rows, columns] = product
        square = jnp.sum(product * product, axis=0, keepdims=True)
        sums.append(jnp.sum(square, axis=1, keepdims=True))

    def left():
        sums.clear()
        from_left(root, side, write)
        return sums[0] + sums[1]

    def right():
        sums.clear()
        from_right(side, root, write)
        return sums[0] + sums[1]

    sums = []
    raw_sum = lax.cond(core == 0, right, left)
    scale = 1.0 / (width * width)
    grad_mean = jnp.sum(grad_sum[...], axis=1, keepdims=True) * scale
    raw_mean = jnp.sum(raw_sum, axis=1, keepdims=True) * scale
    ratio = jnp.sqrt(grad_mean + 1e-06) / jnp.sqrt(raw_mean + 1e-06)
    active = place[1] > 0

    @pl.when(active)
    def _():
        out[...] = (raw[rows_at(core * half, half), :] * ratio).astype(jnp.bfloat16)

    @pl.when(jnp.logical_not(active))
    def _():
        out[...] = own[...]


def place_kernel(targets, place, *refs):
    *pieces, out, sems = refs
    core, plane = place[0], place[2]
    copies = []
    for index, (which, skip, count, shift, start, mine) in enumerate(targets):
        rows = pieces[which].shape[1]
        half = core if mine else 1 - core
        first = lax.rem(plane + shift, 4) * (out.shape[0] // 4) + start
        copies.append(
            pltpu.make_async_copy(
                pieces[which].at[pl.ds(skip, count)],
                out.at[pl.ds(first, count), rows_at(half * rows, rows), :],
                sems.at[index],
            )
        )
    for copy in copies:
        copy.start()
    for copy in copies:
        copy.wait()


def local(partials, owned_block):
    core = lax.axis_index("core")
    plane = lax.axis_index("z")
    slot = lax.axis_index("y") * 4 + lax.axis_index("x")
    _, blocks, piece_rows, width = partials.shape
    planes = 4
    per_plane = blocks // planes
    part = per_plane // 2
    rows = piece_rows // 2
    shards = 16
    half = rows * shards
    swap = [(0, 1), (1, 0)]
    up = [(i, (i + 1) % planes) for i in range(planes)]
    down = [(i, (i - 1) % planes) for i in range(planes)]
    def plus(*terms):
        total = terms[0].astype(jnp.float32)
        for term in terms[1:]:
            total = total + term.astype(jnp.float32)
        return total.astype(jnp.bfloat16)

    smem = pl.BlockSpec(memory_space=pltpu.SMEM)
    vmem = pl.BlockSpec(memory_space=pltpu.VMEM)
    anywhere = pl.BlockSpec(memory_space=pl.ANY)
    halves = partials.reshape(planes, per_plane, 2, rows, width)

    def rows_of(here, shift, which):
        sliced = lax.dynamic_slice(
            halves, ((here + shift) % planes, 0, which, 0, 0), (1, per_plane, 1, rows, width)
        )
        return sliced.reshape(per_plane, rows, width)

    with jax.named_scope("sum_over_replicas"):
        sent, next_plane = lax.optimization_barrier((rows_of(plane, 2, 1 - core), plane))
        got = lax.ppermute(sent, "core", swap)
        kept, *sent = lax.optimization_barrier(
            [rows_of(next_plane, 2, core)] + [rows_of(next_plane, k, 1 - core) for k in (1, 3, 0)]
        )
        got_above, got_below, got_mine = (lax.ppermute(each, "core", swap) for each in sent)
        far = plus(kept, got)
        far_low, far_high, here = lax.optimization_barrier((far[:part], far[part:], plane))
        from_above = lax.ppermute(far_low, "z", down)
        from_below = lax.ppermute(far_high, "z", up)
        kept_above, kept_below, kept_mine = lax.optimization_barrier(
            [rows_of(here, k, core) for k in (1, 3, 0)]
        )
        to_above = plus(kept_above, got_above)
        to_below = plus(kept_below, got_below)
        mine = plus(kept_mine, got_mine)
        low_below = lax.ppermute(to_above[:part], "z", up)
        high_above = lax.ppermute(to_below[part:], "z", down)
        low_below, owners = lax.optimization_barrier((low_below, owned_block))
        low_above = lax.ppermute(plus(to_below[:part], from_above), "z", down)
        high_below = lax.ppermute(plus(to_above[part:], from_below), "z", up)
        summed = jnp.concatenate(
            [
                plus(mine[:part], low_below, low_above),
                plus(mine[part:], high_above, high_below),
                jnp.zeros((shards - per_plane, rows, width), jnp.bfloat16),
            ],
            axis=0,
        )

    block = plane * per_plane + slot
    active = jnp.any(owners == block) & (slot < per_plane)
    place = jnp.stack([core, active.astype(jnp.int32), plane]).astype(jnp.int32)
    summed, place = lax.optimization_barrier((summed, place))

    with jax.named_scope("rows_to_owner"):
        own = lax.all_to_all(summed, ("y", "x"), 0, 0, tiled=True).reshape(half, width)
        sibling = lax.ppermute(own, "core", swap)

    square = (width, width)
    whole = jax.ShapeDtypeStruct(square, jnp.bfloat16)
    work = 2 * width**3
    own_root, grad = pl.pallas_call(
        root_kernel,
        out_shape=[jax.ShapeDtypeStruct((3, half, half), jnp.bfloat16), whole],
        in_specs=[smem, vmem, vmem],
        out_specs=[vmem, vmem],
        scratch_shapes=[
            pltpu.VMEM(square, jnp.float32),
        ]
        + [pltpu.VMEM(square, jnp.bfloat16)] * 4,
        compiler_params=pltpu.CompilerParams(vmem_limit_bytes=40 * mib),
        cost_estimate=pl.CostEstimate(flops=3 * work, bytes_accessed=6 * mib, transcendentals=0),
        name="inverse_root",
    )(place, own, sibling)
    sibling_root = lax.ppermute(own_root, "core", swap)
    side, grad_sum = pl.pallas_call(
        side_kernel,
        out_shape=[whole, jax.ShapeDtypeStruct((1, width), jnp.float32)],
        in_specs=[smem, vmem, vmem],
        out_specs=[vmem, vmem],
        compiler_params=pltpu.CompilerParams(vmem_limit_bytes=32 * mib),
        cost_estimate=pl.CostEstimate(flops=work, bytes_accessed=6 * mib, transcendentals=0),
        name="apply_own_root",
    )(place, own_root, grad)
    finished = pl.pallas_call(
        finish_kernel,
        out_shape=jax.ShapeDtypeStruct((half, width), jnp.bfloat16),
        in_specs=[smem, vmem, vmem, vmem, vmem],
        out_specs=vmem,
        scratch_shapes=[pltpu.VMEM(square, jnp.float32)],
        compiler_params=pltpu.CompilerParams(vmem_limit_bytes=32 * mib),
        cost_estimate=pl.CostEstimate(flops=work, bytes_accessed=6 * mib, transcendentals=0),
        name="apply_other_root",
    )(place, own, side, sibling_root, grad_sum)

    with jax.named_scope("rows_to_shards"):
        back = lax.all_to_all(
            finished.reshape(shards, rows, width), ("y", "x"), 0, 0, tiled=True
        )[:per_plane]

    out_shape = jax.ShapeDtypeStruct((blocks, piece_rows, width), jnp.bfloat16)

    def put(name, before, *entries):
        targets, operands = [], []
        for which, (array, *runs) in enumerate(entries):
            skip = 0
            for shift, start, count, mine in runs:
                targets.append((which, skip, count, shift, start, mine))
                skip += count
            operands.append(array)
        moved = sum(4 * operand.size for operand in operands)
        operands.append(before)
        first = before.shape != out_shape.shape
        return pl.pallas_call(
            functools.partial(place_kernel, targets),
            out_shape=out_shape,
            in_specs=[smem] + [vmem] * len(entries) + [vmem if first else anywhere],
            out_specs=anywhere,
            scratch_shapes=[pltpu.SemaphoreType.DMA((len(targets),))],
            input_output_aliases={} if first else {len(operands): 0},
            compiler_params=pltpu.CompilerParams(vmem_limit_bytes=24 * mib),
            cost_estimate=pl.CostEstimate(flops=0, bytes_accessed=moved, transcendentals=0),
            name=name,
        )(place, *operands)

    def other_core(piece):
        return lax.ppermute(piece, "core", swap)

    with jax.named_scope("gather_over_replicas"):
        above_low = lax.ppermute(back[:part], "z", down)
        below_high = lax.ppermute(back[part:], "z", up)
        behind = other_core(back[:1, :16, :128])
        low, high, behind = lax.optimization_barrier((back[:part], back[part:], behind))
        above_high = lax.ppermute(high, "z", down)
        below_low = lax.ppermute(low, "z", up)
        above_low, below_high, other = lax.optimization_barrier(
            (above_low, below_high, other_core(back))
        )
        far_low = lax.ppermute(above_low, "z", down)
        far_high = lax.ppermute(below_high, "z", up)
        passed = other_core(jnp.concatenate([above_low, below_high], axis=0))
        out = put(
            "place_early",
            behind,
            (back, (0, 0, per_plane, True)),
            (other, (0, 0, per_plane, False)),
            (above_low, (1, 0, part, True)),
            (below_high, (3, part, part, True)),
            (above_high, (1, part, part, True)),
            (below_low, (3, 0, part, True)),
        )
        above_high, below_low, out = lax.optimization_barrier((above_high, below_low, out))
        return put(
            "place_late",
            out,
            (passed, (1, 0, part, False), (3, part, part, False)),
            (other_core(above_high), (1, part, part, False)),
            (other_core(below_low), (3, 0, part, False)),
            (far_low, (2, 0, part, True)),
            (far_high, (2, part, part, True)),
            (other_core(far_low), (2, 0, part, False)),
            (other_core(far_high), (2, part, part, False)),
        )


def solution(mesh):
    grid = Mesh(mesh.devices.reshape(4, 2, 4, 4), ("z", "core", "y", "x"))
    in_specs = (P(("z", "core"), None, ("y", "x"), None), P())
    out_specs = P(None, ("y", "x"), None)
    return jax.shard_map(local, mesh=grid, in_specs=in_specs, out_specs=out_specs, check_vma=False)
```

```python
import functools

import jax
import jax.numpy as jnp
from jax import lax
from jax.experimental import pallas as pl
from jax.experimental.pallas import tpu as pltpu
from jax.sharding import Mesh, PartitionSpec as P

damping = 0.1
mib = 2**20
TILE = 256
ROWS = ((0,), (0,))
COLUMNS = ((1,), (1,))


def dot(a, b, contract=((1,), (0,))):
    return lax.dot_general(a, b, (contract, ((), ())), preferred_element_type=jnp.float32)


def rows_at(start, count):
    return pl.ds(pl.multiple_of(start, count), count)


def add_kernel(one, two, *outs):
    start = 0
    for out in outs:
        run = slice(start, start + out.shape[0])
        out[...] = (one[run].astype(jnp.float32) + two[run].astype(jnp.float32)).astype(out.dtype)
        start += out.shape[0]


def root_kernel(place, own, sibling, root, grad, stat, step, square, coupled, fourth):
    core = place[0]
    half, width = own.shape
    grad[rows_at(core * half, half), :] = own[...]
    grad[rows_at((1 - core) * half, half), :] = sibling[...]
    count = width // TILE
    tiles = [slice(i * TILE, (i + 1) * TILE) for i in range(count)]
    tails = [slice(i * TILE, width) for i in range(count)]
    eye = lax.broadcasted_iota(jnp.int32, (TILE, TILE), 0) == lax.broadcasted_iota(
        jnp.int32, (TILE, TILE), 1
    )

    def squares(value):
        return jnp.sum(value * value, axis=0, keepdims=True)

    def add_up(value):
        return jnp.sum(value, axis=1, keepdims=True)

    def statistic(contract):
        total = jnp.zeros((1, 1), jnp.float32)
        for i in range(count):
            if contract == ROWS:
                product = dot(grad[:, tiles[i]], grad[:, tails[i]], ROWS)
            else:
                product = dot(grad[tiles[i], :], grad[tails[i], :], COLUMNS)
            value = product * (1.0 / width)
            block = value[:, :TILE] + jnp.where(eye, damping, 0.0)
            stat[tiles[i], tiles[i]] = block
            total = total + add_up(squares(block))
            if i + 1 < count:
                stat[tiles[i], tails[i + 1]] = value[:, TILE:]
                total = total + 2.0 * add_up(squares(value[:, TILE:]))
        return total

    total = lax.cond(core == 0, lambda: statistic(COLUMNS), lambda: statistic(ROWS))
    inverse = 4.0 * lax.rsqrt(total)

    def rest(matrix, i):
        if i + 1 < count:
            matrix[tails[i + 1], tiles[i]] = matrix[tiles[i], tails[i + 1]].T

    across, along = [], []
    for i in range(count):
        matrix = (stat[tiles[i], tails[i]] * inverse).astype(jnp.bfloat16).astype(jnp.float32)
        block = matrix[:, :TILE]
        value = ((jnp.where(eye, 5.0, 0.0) - block) * 0.25).astype(jnp.bfloat16)
        both = jnp.where(eye, 4.0 * value.astype(jnp.float32) + block, 0.0)
        across.append(jnp.sum(both, axis=0, keepdims=True))
        along.append(jnp.sum(both, axis=1, keepdims=True))
        step[tiles[i], tiles[i]] = value
        if i + 1 < count:
            step[tiles[i], tails[i + 1]] = (matrix[:, TILE:] * -0.25).astype(jnp.bfloat16)
            rest(step, i)
    across = jnp.concatenate(across, axis=1)
    for i in range(count):
        product = dot(step[tiles[i], :], step[:, tails[i]])
        square[tiles[i], tails[i]] = product.astype(jnp.bfloat16)
        rest(square, i)
        value = step[tiles[i], tails[i]].astype(jnp.float32)
        coupled[tiles[i], tails[i]] = (value * across[:, tails[i]] - 4.0 * product).astype(
            jnp.bfloat16
        )
        if i + 1 < count:
            below = value[:, TILE:] * along[i] - 4.0 * product[:, TILE:]
            coupled[tails[i + 1], tiles[i]] = below.astype(jnp.bfloat16).T
    for i in range(count):
        product = dot(square[tiles[i], :], square[:, tails[i]])
        fourth[tiles[i], tails[i]] = product.astype(jnp.bfloat16)
        rest(fourth, i)
    for i in range(count):
        product = dot(fourth[tiles[i], :], coupled[:, tails[i]])
        value = step[tiles[i], tails[i]].astype(jnp.float32)
        value = ((5.0 * value - product) * 0.25).astype(jnp.bfloat16)
        start = i * TILE
        if start < half:
            root[0, tiles[i], start:half] = value[:, : half - start]
            root[1, tiles[i], :] = value[:, half - start :]
            if start + TILE < half:
                root[0, start + TILE : half, tiles[i]] = value[:, TILE : half - start].T
        else:
            rows, columns = slice(start - half, start - half + TILE), slice(start - half, half)
            root[2, rows, columns] = value
            if start + TILE < width:
                root[2, start - half + TILE : half, rows] = value[:, TILE:].T


def from_left(root, matrix, write):
    half = root.shape[1]
    one, two, three = root[0], root[1], root[2]
    top, bottom = matrix[:half, :], matrix[half:, :]
    write(slice(0, half), slice(None), dot(one, top) + dot(two, bottom))
    write(slice(half, 2 * half), slice(None), dot(two, top, ROWS) + dot(three, bottom))


def from_right(matrix, root, write):
    half = root.shape[1]
    one, two, three = root[0], root[1], root[2]
    before, after = matrix[:, :half], matrix[:, half:]
    write(slice(None), slice(0, half), dot(before, one) + dot(after, two, COLUMNS))
    write(slice(None), slice(half, 2 * half), dot(before, two) + dot(after, three))


def side_kernel(place, root, grad, side, grad_sum):
    core = place[0]

    def write(rows, columns, product):
        side[rows, columns] = product.astype(jnp.bfloat16)

    @pl.when(core == 0)
    def _():
        from_left(root, grad, write)

    @pl.when(core == 1)
    def _():
        from_right(grad, root, write)

    value = grad[...].astype(jnp.float32)
    grad_sum[...] = jnp.sum(value * value, axis=0, keepdims=True)


def finish_kernel(place, own, side, root, grad_sum, out, raw):
    core = place[0]
    half, width = own.shape

    def write(rows, columns, product):
        raw[rows, columns] = product
        square = jnp.sum(product * product, axis=0, keepdims=True)
        sums.append(jnp.sum(square, axis=1, keepdims=True))

    def left():
        sums.clear()
        from_left(root, side, write)
        return sums[0] + sums[1]

    def right():
        sums.clear()
        from_right(side, root, write)
        return sums[0] + sums[1]

    sums = []
    raw_sum = lax.cond(core == 0, right, left)
    scale = 1.0 / (width * width)
    grad_mean = jnp.sum(grad_sum[...], axis=1, keepdims=True) * scale
    raw_mean = jnp.sum(raw_sum, axis=1, keepdims=True) * scale
    ratio = jnp.sqrt(grad_mean + 1e-06) / jnp.sqrt(raw_mean + 1e-06)
    active = place[1] > 0

    @pl.when(active)
    def _():
        out[...] = (raw[rows_at(core * half, half), :] * ratio).astype(jnp.bfloat16)

    @pl.when(jnp.logical_not(active))
    def _():
        out[...] = own[...]


def place_kernel(targets, place, *refs):
    *pieces, out, sems = refs
    core, plane = place[0], place[2]
    copies = []
    for index, (which, skip, count, shift, start, mine) in enumerate(targets):
        rows = pieces[which].shape[1]
        half = core if mine else 1 - core
        first = lax.rem(plane + shift, 4) * (out.shape[0] // 4) + start
        copies.append(
            pltpu.make_async_copy(
                pieces[which].at[pl.ds(skip, count)],
                out.at[pl.ds(first, count), rows_at(half * rows, rows), :],
                sems.at[index],
            )
        )
    for copy in copies:
        copy.start()
    for copy in copies:
        copy.wait()


def local(partials, owned_block):
    core = lax.axis_index("core")
    plane = lax.axis_index("z")
    slot = lax.axis_index("y") * 4 + lax.axis_index("x")
    _, blocks, piece_rows, width = partials.shape
    planes = 4
    per_plane = blocks // planes
    part = per_plane // 2
    rows = piece_rows // 2
    shards = 16
    half = rows * shards
    swap = [(0, 1), (1, 0)]
    up = [(i, (i + 1) % planes) for i in range(planes)]
    down = [(i, (i - 1) % planes) for i in range(planes)]
    def plus(*terms):
        total = terms[0].astype(jnp.float32)
        for term in terms[1:]:
            total = total + term.astype(jnp.float32)
        return total.astype(jnp.bfloat16)

    smem = pl.BlockSpec(memory_space=pltpu.SMEM)
    vmem = pl.BlockSpec(memory_space=pltpu.VMEM)
    anywhere = pl.BlockSpec(memory_space=pl.ANY)
    halves = partials.reshape(planes, per_plane, 2, rows, width)

    def rows_of(here, shift, which):
        sliced = lax.dynamic_slice(
            halves, ((here + shift) % planes, 0, which, 0, 0), (1, per_plane, 1, rows, width)
        )
        return sliced.reshape(per_plane, rows, width)

    with jax.named_scope("sum_over_replicas"):
        sent, next_plane = lax.optimization_barrier((rows_of(plane, 2, 1 - core), plane))
        got = lax.ppermute(sent, "core", swap)
        kept, *sent = lax.optimization_barrier(
            [rows_of(next_plane, 2, core)] + [rows_of(next_plane, k, 1 - core) for k in (1, 3, 0)]
        )
        got_above, got_below, got_mine = (lax.ppermute(each, "core", swap) for each in sent)
        far_low, far_high = pl.pallas_call(
            add_kernel,
            out_shape=[jax.ShapeDtypeStruct((part, rows, width), jnp.bfloat16)] * 2,
            in_specs=[vmem] * 2,
            out_specs=[vmem] * 2,
            compiler_params=pltpu.CompilerParams(vmem_limit_bytes=8 * mib),
            cost_estimate=pl.CostEstimate(
                flops=kept.size, bytes_accessed=6 * kept.size, transcendentals=0
            ),
            name="add_rows",
        )(kept, got)
        far_low, far_high, here = lax.optimization_barrier((far_low, far_high, plane))
        from_above = lax.ppermute(far_low, "z", down)
        from_below = lax.ppermute(far_high, "z", up)
        kept_above, kept_below, kept_mine = lax.optimization_barrier(
            [rows_of(here, k, core) for k in (1, 3, 0)]
        )
        to_above = plus(kept_above, got_above)
        to_below = plus(kept_below, got_below)
        mine = plus(kept_mine, got_mine)
        low_below = lax.ppermute(to_above[:part], "z", up)
        high_above = lax.ppermute(to_below[part:], "z", down)
        low_below, owners = lax.optimization_barrier((low_below, owned_block))
        low_above = lax.ppermute(plus(to_below[:part], from_above), "z", down)
        high_below = lax.ppermute(plus(to_above[part:], from_below), "z", up)
        summed = jnp.concatenate(
            [
                plus(mine[:part], low_below, low_above),
                plus(mine[part:], high_above, high_below),
                jnp.zeros((shards - per_plane, rows, width), jnp.bfloat16),
            ],
            axis=0,
        )

    block = plane * per_plane + slot
    active = jnp.any(owners == block) & (slot < per_plane)
    place = jnp.stack([core, active.astype(jnp.int32), plane]).astype(jnp.int32)
    summed, place = lax.optimization_barrier((summed, place))

    with jax.named_scope("rows_to_owner"):
        own = lax.all_to_all(summed, ("y", "x"), 0, 0, tiled=True).reshape(half, width)
        sibling = lax.ppermute(own, "core", swap)

    square = (width, width)
    whole = jax.ShapeDtypeStruct(square, jnp.bfloat16)
    work = 2 * width**3
    own_root, grad = pl.pallas_call(
        root_kernel,
        out_shape=[jax.ShapeDtypeStruct((3, half, half), jnp.bfloat16), whole],
        in_specs=[smem, vmem, vmem],
        out_specs=[vmem, vmem],
        scratch_shapes=[
            pltpu.VMEM(square, jnp.float32),
        ]
        + [pltpu.VMEM(square, jnp.bfloat16)] * 4,
        compiler_params=pltpu.CompilerParams(vmem_limit_bytes=40 * mib),
        cost_estimate=pl.CostEstimate(flops=3 * work, bytes_accessed=6 * mib, transcendentals=0),
        name="inverse_root",
    )(place, own, sibling)
    sibling_root = lax.ppermute(own_root, "core", swap)
    side, grad_sum = pl.pallas_call(
        side_kernel,
        out_shape=[whole, jax.ShapeDtypeStruct((1, width), jnp.float32)],
        in_specs=[smem, vmem, vmem],
        out_specs=[vmem, vmem],
        compiler_params=pltpu.CompilerParams(vmem_limit_bytes=32 * mib),
        cost_estimate=pl.CostEstimate(flops=work, bytes_accessed=6 * mib, transcendentals=0),
        name="apply_own_root",
    )(place, own_root, grad)
    finished = pl.pallas_call(
        finish_kernel,
        out_shape=jax.ShapeDtypeStruct((half, width), jnp.bfloat16),
        in_specs=[smem, vmem, vmem, vmem, vmem],
        out_specs=vmem,
        scratch_shapes=[pltpu.VMEM(square, jnp.float32)],
        compiler_params=pltpu.CompilerParams(vmem_limit_bytes=32 * mib),
        cost_estimate=pl.CostEstimate(flops=work, bytes_accessed=6 * mib, transcendentals=0),
        name="apply_other_root",
    )(place, own, side, sibling_root, grad_sum)

    with jax.named_scope("rows_to_shards"):
        back = lax.all_to_all(
            finished.reshape(shards, rows, width), ("y", "x"), 0, 0, tiled=True
        )[:per_plane]

    out_shape = jax.ShapeDtypeStruct((blocks, piece_rows, width), jnp.bfloat16)

    def put(name, before, *entries):
        targets, operands = [], []
        for which, (array, *runs) in enumerate(entries):
            skip = 0
            for shift, start, count, mine in runs:
                targets.append((which, skip, count, shift, start, mine))
                skip += count
            operands.append(array)
        moved = sum(4 * operand.size for operand in operands)
        operands.append(before)
        first = before.shape != out_shape.shape
        return pl.pallas_call(
            functools.partial(place_kernel, targets),
            out_shape=out_shape,
            in_specs=[smem] + [vmem] * len(entries) + [vmem if first else anywhere],
            out_specs=anywhere,
            scratch_shapes=[pltpu.SemaphoreType.DMA((len(targets),))],
            input_output_aliases={} if first else {len(operands): 0},
            compiler_params=pltpu.CompilerParams(vmem_limit_bytes=24 * mib),
            cost_estimate=pl.CostEstimate(flops=0, bytes_accessed=moved, transcendentals=0),
            name=name,
        )(place, *operands)

    def other_core(piece):
        return lax.ppermute(piece, "core", swap)

    with jax.named_scope("gather_over_replicas"):
        above_low = lax.ppermute(back[:part], "z", down)
        below_high = lax.ppermute(back[part:], "z", up)
        behind = other_core(back[:1, :16, :128])
        low, high, behind = lax.optimization_barrier((back[:part], back[part:], behind))
        above_high = lax.ppermute(high, "z", down)
        below_low = lax.ppermute(low, "z", up)
        above_low, below_high, other = lax.optimization_barrier(
            (above_low, below_high, other_core(back))
        )
        far_low = lax.ppermute(above_low, "z", down)
        far_high = lax.ppermute(below_high, "z", up)
        passed = other_core(jnp.concatenate([above_low, below_high], axis=0))
        out = put(
            "place_early",
            behind,
            (back, (0, 0, per_plane, True)),
            (other, (0, 0, per_plane, False)),
            (above_low, (1, 0, part, True)),
            (below_high, (3, part, part, True)),
            (above_high, (1, part, part, True)),
            (below_low, (3, 0, part, True)),
        )
        above_high, below_low, out = lax.optimization_barrier((above_high, below_low, out))
        return put(
            "place_late",
            out,
            (passed, (1, 0, part, False), (3, part, part, False)),
            (other_core(above_high), (1, part, part, False)),
            (other_core(below_low), (3, 0, part, False)),
            (far_low, (2, 0, part, True)),
            (far_high, (2, part, part, True)),
            (other_core(far_low), (2, 0, part, False)),
            (other_core(far_high), (2, part, part, False)),
        )


def solution(mesh):
    grid = Mesh(mesh.devices.reshape(4, 2, 4, 4), ("z", "core", "y", "x"))
    in_specs = (P(("z", "core"), None, ("y", "x"), None), P())
    out_specs = P(None, ("y", "x"), None)
    return jax.shard_map(local, mesh=grid, in_specs=in_specs, out_specs=out_specs, check_vma=False)
```

```python
import functools

import jax
import jax.numpy as jnp
from jax import lax
from jax.experimental import pallas as pl
from jax.experimental.pallas import tpu as pltpu
from jax.sharding import Mesh, PartitionSpec as P

damping = 0.1
mib = 2**20
TILE = 256
FETCH_VMEM = 47 * mib
ROWS = ((0,), (0,))
COLUMNS = ((1,), (1,))


def dot(a, b, contract=((1,), (0,))):
    return lax.dot_general(a, b, (contract, ((), ())), preferred_element_type=jnp.float32)


def rows_at(start, count):
    return pl.ds(pl.multiple_of(start, count), count)


def fetch_kernel(wanted, place, source, *refs):
    *outs, sems = refs
    core, plane = place[0], place[1]
    copies = []
    for index, (out, (shift, mine)) in enumerate(zip(outs, wanted)):
        count, rows, _ = out.shape
        half = core if mine else 1 - core
        first = lax.rem(plane + shift, 4) * count
        copies.append(
            pltpu.make_async_copy(
                source.at[0, pl.ds(first, count), rows_at(half * rows, rows), :], out, sems.at[index]
            )
        )
    for copy in copies:
        copy.start()
    for copy in copies:
        copy.wait()


def add_kernel(one, two, *outs):
    start = 0
    for out in outs:
        run = slice(start, start + out.shape[0])
        out[...] = (one[run].astype(jnp.float32) + two[run].astype(jnp.float32)).astype(out.dtype)
        start += out.shape[0]


def root_kernel(place, own, sibling, root, grad, stat, step, square, coupled, fourth):
    core = place[0]
    half, width = own.shape
    grad[rows_at(core * half, half), :] = own[...]
    grad[rows_at((1 - core) * half, half), :] = sibling[...]
    count = width // TILE
    tiles = [slice(i * TILE, (i + 1) * TILE) for i in range(count)]
    tails = [slice(i * TILE, width) for i in range(count)]
    eye = lax.broadcasted_iota(jnp.int32, (TILE, TILE), 0) == lax.broadcasted_iota(
        jnp.int32, (TILE, TILE), 1
    )

    def squares(value):
        return jnp.sum(value * value, axis=0, keepdims=True)

    def add_up(value):
        return jnp.sum(value, axis=1, keepdims=True)

    def statistic(contract):
        total = jnp.zeros((1, 1), jnp.float32)
        for i in range(count):
            if contract == ROWS:
                product = dot(grad[:, tiles[i]], grad[:, tails[i]], ROWS)
            else:
                product = dot(grad[tiles[i], :], grad[tails[i], :], COLUMNS)
            value = product * (1.0 / width)
            block = value[:, :TILE] + jnp.where(eye, damping, 0.0)
            stat[tiles[i], tiles[i]] = block
            total = total + add_up(squares(block))
            if i + 1 < count:
                stat[tiles[i], tails[i + 1]] = value[:, TILE:]
                total = total + 2.0 * add_up(squares(value[:, TILE:]))
        return total

    total = lax.cond(core == 0, lambda: statistic(COLUMNS), lambda: statistic(ROWS))
    inverse = 4.0 * lax.rsqrt(total)

    def rest(matrix, i):
        if i + 1 < count:
            matrix[tails[i + 1], tiles[i]] = matrix[tiles[i], tails[i + 1]].T

    across, along = [], []
    for i in range(count):
        matrix = (stat[tiles[i], tails[i]] * inverse).astype(jnp.bfloat16).astype(jnp.float32)
        block = matrix[:, :TILE]
        value = ((jnp.where(eye, 5.0, 0.0) - block) * 0.25).astype(jnp.bfloat16)
        both = jnp.where(eye, 4.0 * value.astype(jnp.float32) + block, 0.0)
        across.append(jnp.sum(both, axis=0, keepdims=True))
        along.append(jnp.sum(both, axis=1, keepdims=True))
        step[tiles[i], tiles[i]] = value
        if i + 1 < count:
            step[tiles[i], tails[i + 1]] = (matrix[:, TILE:] * -0.25).astype(jnp.bfloat16)
            rest(step, i)
    across = jnp.concatenate(across, axis=1)
    for i in range(count):
        product = dot(step[tiles[i], :], step[:, tails[i]])
        square[tiles[i], tails[i]] = product.astype(jnp.bfloat16)
        rest(square, i)
        value = step[tiles[i], tails[i]].astype(jnp.float32)
        coupled[tiles[i], tails[i]] = (value * across[:, tails[i]] - 4.0 * product).astype(
            jnp.bfloat16
        )
        if i + 1 < count:
            below = value[:, TILE:] * along[i] - 4.0 * product[:, TILE:]
            coupled[tails[i + 1], tiles[i]] = below.astype(jnp.bfloat16).T
    for i in range(count):
        product = dot(square[tiles[i], :], square[:, tails[i]])
        fourth[tiles[i], tails[i]] = product.astype(jnp.bfloat16)
        rest(fourth, i)
    for i in range(count):
        product = dot(fourth[tiles[i], :], coupled[:, tails[i]])
        value = step[tiles[i], tails[i]].astype(jnp.float32)
        value = ((5.0 * value - product) * 0.25).astype(jnp.bfloat16)
        start = i * TILE
        if start < half:
            root[0, tiles[i], start:half] = value[:, : half - start]
            root[1, tiles[i], :] = value[:, half - start :]
            if start + TILE < half:
                root[0, start + TILE : half, tiles[i]] = value[:, TILE : half - start].T
        else:
            rows, columns = slice(start - half, start - half + TILE), slice(start - half, half)
            root[2, rows, columns] = value
            if start + TILE < width:
                root[2, start - half + TILE : half, rows] = value[:, TILE:].T


def from_left(root, matrix, write):
    half = root.shape[1]
    one, two, three = root[0], root[1], root[2]
    top, bottom = matrix[:half, :], matrix[half:, :]
    write(slice(0, half), slice(None), dot(one, top) + dot(two, bottom))
    write(slice(half, 2 * half), slice(None), dot(two, top, ROWS) + dot(three, bottom))


def from_right(matrix, root, write):
    half = root.shape[1]
    one, two, three = root[0], root[1], root[2]
    before, after = matrix[:, :half], matrix[:, half:]
    write(slice(None), slice(0, half), dot(before, one) + dot(after, two, COLUMNS))
    write(slice(None), slice(half, 2 * half), dot(before, two) + dot(after, three))


def side_kernel(place, root, grad, side, grad_sum):
    core = place[0]

    def write(rows, columns, product):
        side[rows, columns] = product.astype(jnp.bfloat16)

    @pl.when(core == 0)
    def _():
        from_left(root, grad, write)

    @pl.when(core == 1)
    def _():
        from_right(grad, root, write)

    value = grad[...].astype(jnp.float32)
    grad_sum[...] = jnp.sum(value * value, axis=0, keepdims=True)


def finish_kernel(place, own, side, root, grad_sum, out, raw):
    core = place[0]
    half, width = own.shape

    def write(rows, columns, product):
        raw[rows, columns] = product
        square = jnp.sum(product * product, axis=0, keepdims=True)
        sums.append(jnp.sum(square, axis=1, keepdims=True))

    def left():
        sums.clear()
        from_left(root, side, write)
        return sums[0] + sums[1]

    def right():
        sums.clear()
        from_right(side, root, write)
        return sums[0] + sums[1]

    sums = []
    raw_sum = lax.cond(core == 0, right, left)
    scale = 1.0 / (width * width)
    grad_mean = jnp.sum(grad_sum[...], axis=1, keepdims=True) * scale
    raw_mean = jnp.sum(raw_sum, axis=1, keepdims=True) * scale
    ratio = jnp.sqrt(grad_mean + 1e-06) / jnp.sqrt(raw_mean + 1e-06)
    active = place[1] > 0

    @pl.when(active)
    def _():
        out[...] = (raw[rows_at(core * half, half), :] * ratio).astype(jnp.bfloat16)

    @pl.when(jnp.logical_not(active))
    def _():
        out[...] = own[...]


def place_kernel(targets, place, *refs):
    *pieces, out, sems = refs
    core, plane = place[0], place[2]
    copies = []
    for index, (which, skip, count, shift, start, mine) in enumerate(targets):
        rows = pieces[which].shape[1]
        half = core if mine else 1 - core
        first = lax.rem(plane + shift, 4) * (out.shape[0] // 4) + start
        copies.append(
            pltpu.make_async_copy(
                pieces[which].at[pl.ds(skip, count)],
                out.at[pl.ds(first, count), rows_at(half * rows, rows), :],
                sems.at[index],
            )
        )
    for copy in copies:
        copy.start()
    for copy in copies:
        copy.wait()


def local(partials, owned_block):
    core = lax.axis_index("core")
    plane = lax.axis_index("z")
    slot = lax.axis_index("y") * 4 + lax.axis_index("x")
    _, blocks, piece_rows, width = partials.shape
    planes = 4
    per_plane = blocks // planes
    part = per_plane // 2
    rows = piece_rows // 2
    shards = 16
    half = rows * shards
    swap = [(0, 1), (1, 0)]
    up = [(i, (i + 1) % planes) for i in range(planes)]
    down = [(i, (i - 1) % planes) for i in range(planes)]
    def plus(*terms):
        total = terms[0].astype(jnp.float32)
        for term in terms[1:]:
            total = total + term.astype(jnp.float32)
        return total.astype(jnp.bfloat16)

    smem = pl.BlockSpec(memory_space=pltpu.SMEM)
    vmem = pl.BlockSpec(memory_space=pltpu.VMEM)
    anywhere = pl.BlockSpec(memory_space=pl.ANY)
    halves = partials.reshape(planes, per_plane, 2, rows, width)

    def rows_of(here, shift, which):
        sliced = lax.dynamic_slice(
            halves, ((here + shift) % planes, 0, which, 0, 0), (1, per_plane, 1, rows, width)
        )
        return sliced.reshape(per_plane, rows, width)

    with jax.named_scope("sum_over_replicas"):
        sent, next_plane = lax.optimization_barrier((rows_of(plane, 2, 1 - core), plane))
        got = lax.ppermute(sent, "core", swap)
        plane_rows = jax.ShapeDtypeStruct((per_plane, rows, width), jnp.bfloat16)
        kept, *sent = pl.pallas_call(
            functools.partial(fetch_kernel, ((2, True), (1, False), (3, False), (0, False))),
            out_shape=[plane_rows] * 4,
            in_specs=[smem, anywhere],
            out_specs=[vmem] * 4,
            scratch_shapes=[pltpu.SemaphoreType.DMA((4,))],
            compiler_params=pltpu.CompilerParams(vmem_limit_bytes=FETCH_VMEM),
            cost_estimate=pl.CostEstimate(
                flops=0, bytes_accessed=16 * plane_rows.size, transcendentals=0
            ),
            name="fetch_rows",
        )(jnp.stack([core, next_plane]).astype(jnp.int32), partials)
        got_above, got_below, got_mine = (lax.ppermute(each, "core", swap) for each in sent)
        far_low, far_high = pl.pallas_call(
            add_kernel,
            out_shape=[jax.ShapeDtypeStruct((part, rows, width), jnp.bfloat16)] * 2,
            in_specs=[vmem] * 2,
            out_specs=[vmem] * 2,
            compiler_params=pltpu.CompilerParams(vmem_limit_bytes=8 * mib),
            cost_estimate=pl.CostEstimate(
                flops=kept.size, bytes_accessed=6 * kept.size, transcendentals=0
            ),
            name="add_rows",
        )(kept, got)
        far_low, far_high, here = lax.optimization_barrier((far_low, far_high, plane))
        from_above = lax.ppermute(far_low, "z", down)
        from_below = lax.ppermute(far_high, "z", up)
        kept_above, kept_below, kept_mine = lax.optimization_barrier(
            [rows_of(here, k, core) for k in (1, 3, 0)]
        )
        to_above = plus(kept_above, got_above)
        to_below = plus(kept_below, got_below)
        mine = plus(kept_mine, got_mine)
        low_below = lax.ppermute(to_above[:part], "z", up)
        high_above = lax.ppermute(to_below[part:], "z", down)
        low_below, owners = lax.optimization_barrier((low_below, owned_block))
        low_above = lax.ppermute(plus(to_below[:part], from_above), "z", down)
        high_below = lax.ppermute(plus(to_above[part:], from_below), "z", up)
        summed = jnp.concatenate(
            [
                plus(mine[:part], low_below, low_above),
                plus(mine[part:], high_above, high_below),
                jnp.zeros((shards - per_plane, rows, width), jnp.bfloat16),
            ],
            axis=0,
        )

    block = plane * per_plane + slot
    active = jnp.any(owners == block) & (slot < per_plane)
    place = jnp.stack([core, active.astype(jnp.int32), plane]).astype(jnp.int32)
    summed, place = lax.optimization_barrier((summed, place))

    with jax.named_scope("rows_to_owner"):
        own = lax.all_to_all(summed, ("y", "x"), 0, 0, tiled=True).reshape(half, width)
        sibling = lax.ppermute(own, "core", swap)

    square = (width, width)
    whole = jax.ShapeDtypeStruct(square, jnp.bfloat16)
    work = 2 * width**3
    own_root, grad = pl.pallas_call(
        root_kernel,
        out_shape=[jax.ShapeDtypeStruct((3, half, half), jnp.bfloat16), whole],
        in_specs=[smem, vmem, vmem],
        out_specs=[vmem, vmem],
        scratch_shapes=[
            pltpu.VMEM(square, jnp.float32),
        ]
        + [pltpu.VMEM(square, jnp.bfloat16)] * 4,
        compiler_params=pltpu.CompilerParams(vmem_limit_bytes=40 * mib),
        cost_estimate=pl.CostEstimate(flops=3 * work, bytes_accessed=6 * mib, transcendentals=0),
        name="inverse_root",
    )(place, own, sibling)
    sibling_root = lax.ppermute(own_root, "core", swap)
    side, grad_sum = pl.pallas_call(
        side_kernel,
        out_shape=[whole, jax.ShapeDtypeStruct((1, width), jnp.float32)],
        in_specs=[smem, vmem, vmem],
        out_specs=[vmem, vmem],
        compiler_params=pltpu.CompilerParams(vmem_limit_bytes=32 * mib),
        cost_estimate=pl.CostEstimate(flops=work, bytes_accessed=6 * mib, transcendentals=0),
        name="apply_own_root",
    )(place, own_root, grad)
    finished = pl.pallas_call(
        finish_kernel,
        out_shape=jax.ShapeDtypeStruct((half, width), jnp.bfloat16),
        in_specs=[smem, vmem, vmem, vmem, vmem],
        out_specs=vmem,
        scratch_shapes=[pltpu.VMEM(square, jnp.float32)],
        compiler_params=pltpu.CompilerParams(vmem_limit_bytes=32 * mib),
        cost_estimate=pl.CostEstimate(flops=work, bytes_accessed=6 * mib, transcendentals=0),
        name="apply_other_root",
    )(place, own, side, sibling_root, grad_sum)

    with jax.named_scope("rows_to_shards"):
        back = lax.all_to_all(
            finished.reshape(shards, rows, width), ("y", "x"), 0, 0, tiled=True
        )[:per_plane]

    out_shape = jax.ShapeDtypeStruct((blocks, piece_rows, width), jnp.bfloat16)

    def put(name, before, *entries):
        targets, operands = [], []
        for which, (array, *runs) in enumerate(entries):
            skip = 0
            for shift, start, count, mine in runs:
                targets.append((which, skip, count, shift, start, mine))
                skip += count
            operands.append(array)
        moved = sum(4 * operand.size for operand in operands)
        operands.append(before)
        first = before.shape != out_shape.shape
        return pl.pallas_call(
            functools.partial(place_kernel, targets),
            out_shape=out_shape,
            in_specs=[smem] + [vmem] * len(entries) + [vmem if first else anywhere],
            out_specs=anywhere,
            scratch_shapes=[pltpu.SemaphoreType.DMA((len(targets),))],
            input_output_aliases={} if first else {len(operands): 0},
            compiler_params=pltpu.CompilerParams(vmem_limit_bytes=24 * mib),
            cost_estimate=pl.CostEstimate(flops=0, bytes_accessed=moved, transcendentals=0),
            name=name,
        )(place, *operands)

    def other_core(piece):
        return lax.ppermute(piece, "core", swap)

    with jax.named_scope("gather_over_replicas"):
        above_low = lax.ppermute(back[:part], "z", down)
        below_high = lax.ppermute(back[part:], "z", up)
        behind = other_core(back[:1, :16, :128])
        low, high, behind = lax.optimization_barrier((back[:part], back[part:], behind))
        above_high = lax.ppermute(high, "z", down)
        below_low = lax.ppermute(low, "z", up)
        above_low, below_high, other = lax.optimization_barrier(
            (above_low, below_high, other_core(back))
        )
        far_low = lax.ppermute(above_low, "z", down)
        far_high = lax.ppermute(below_high, "z", up)
        passed = other_core(jnp.concatenate([above_low, below_high], axis=0))
        out = put(
            "place_early",
            behind,
            (back, (0, 0, per_plane, True)),
            (other, (0, 0, per_plane, False)),
            (above_low, (1, 0, part, True)),
            (below_high, (3, part, part, True)),
            (above_high, (1, part, part, True)),
            (below_low, (3, 0, part, True)),
        )
        above_high, below_low, out = lax.optimization_barrier((above_high, below_low, out))
        return put(
            "place_late",
            out,
            (passed, (1, 0, part, False), (3, part, part, False)),
            (other_core(above_high), (1, part, part, False)),
            (other_core(below_low), (3, 0, part, False)),
            (far_low, (2, 0, part, True)),
            (far_high, (2, part, part, True)),
            (other_core(far_low), (2, 0, part, False)),
            (other_core(far_high), (2, part, part, False)),
        )


def solution(mesh):
    grid = Mesh(mesh.devices.reshape(4, 2, 4, 4), ("z", "core", "y", "x"))
    in_specs = (P(("z", "core"), None, ("y", "x"), None), P())
    out_specs = P(None, ("y", "x"), None)
    return jax.shard_map(local, mesh=grid, in_specs=in_specs, out_specs=out_specs, check_vma=False)
```

```python
import functools

import jax
import jax.numpy as jnp
from jax import lax
from jax.experimental import pallas as pl
from jax.experimental.pallas import tpu as pltpu
from jax.sharding import Mesh, PartitionSpec as P

damping = 0.1
mib = 2**20
TILE = 256
ROWS = ((0,), (0,))
COLUMNS = ((1,), (1,))


def dot(a, b, contract=((1,), (0,))):
    return lax.dot_general(a, b, (contract, ((), ())), preferred_element_type=jnp.float32)


def rows_at(start, count):
    return pl.ds(pl.multiple_of(start, count), count)


def add_kernel(one, two, *outs):
    start = 0
    for out in outs:
        run = slice(start, start + out.shape[0])
        out[...] = (one[run].astype(jnp.float32) + two[run].astype(jnp.float32)).astype(out.dtype)
        start += out.shape[0]


def sum_kernel(mine, low_below, low_above, high_above, high_below, out):
    count, part = mine.shape[0], low_below.shape[0]
    for run, one, two in (
        (slice(0, part), low_below, low_above),
        (slice(part, count), high_above, high_below),
    ):
        total = mine[run].astype(jnp.float32) + one[...].astype(jnp.float32)
        out[run] = (total + two[...].astype(jnp.float32)).astype(out.dtype)
    out[count:] = jnp.zeros((out.shape[0] - count, *out.shape[1:]), out.dtype)


def root_kernel(place, own, sibling, root, grad, stat, step, square, coupled, fourth):
    core = place[0]
    half, width = own.shape
    grad[rows_at(core * half, half), :] = own[...]
    grad[rows_at((1 - core) * half, half), :] = sibling[...]
    count = width // TILE
    tiles = [slice(i * TILE, (i + 1) * TILE) for i in range(count)]
    tails = [slice(i * TILE, width) for i in range(count)]
    eye = lax.broadcasted_iota(jnp.int32, (TILE, TILE), 0) == lax.broadcasted_iota(
        jnp.int32, (TILE, TILE), 1
    )

    def squares(value):
        return jnp.sum(value * value, axis=0, keepdims=True)

    def add_up(value):
        return jnp.sum(value, axis=1, keepdims=True)

    def statistic(contract):
        total = jnp.zeros((1, 1), jnp.float32)
        for i in range(count):
            if contract == ROWS:
                product = dot(grad[:, tiles[i]], grad[:, tails[i]], ROWS)
            else:
                product = dot(grad[tiles[i], :], grad[tails[i], :], COLUMNS)
            value = product * (1.0 / width)
            block = value[:, :TILE] + jnp.where(eye, damping, 0.0)
            stat[tiles[i], tiles[i]] = block
            total = total + add_up(squares(block))
            if i + 1 < count:
                stat[tiles[i], tails[i + 1]] = value[:, TILE:]
                total = total + 2.0 * add_up(squares(value[:, TILE:]))
        return total

    total = lax.cond(core == 0, lambda: statistic(COLUMNS), lambda: statistic(ROWS))
    inverse = 4.0 * lax.rsqrt(total)

    def rest(matrix, i):
        if i + 1 < count:
            matrix[tails[i + 1], tiles[i]] = matrix[tiles[i], tails[i + 1]].T

    across, along = [], []
    for i in range(count):
        matrix = (stat[tiles[i], tails[i]] * inverse).astype(jnp.bfloat16).astype(jnp.float32)
        block = matrix[:, :TILE]
        value = ((jnp.where(eye, 5.0, 0.0) - block) * 0.25).astype(jnp.bfloat16)
        both = jnp.where(eye, 4.0 * value.astype(jnp.float32) + block, 0.0)
        across.append(jnp.sum(both, axis=0, keepdims=True))
        along.append(jnp.sum(both, axis=1, keepdims=True))
        step[tiles[i], tiles[i]] = value
        if i + 1 < count:
            step[tiles[i], tails[i + 1]] = (matrix[:, TILE:] * -0.25).astype(jnp.bfloat16)
            rest(step, i)
    across = jnp.concatenate(across, axis=1)
    for i in range(count):
        product = dot(step[tiles[i], :], step[:, tails[i]])
        square[tiles[i], tails[i]] = product.astype(jnp.bfloat16)
        rest(square, i)
        value = step[tiles[i], tails[i]].astype(jnp.float32)
        coupled[tiles[i], tails[i]] = (value * across[:, tails[i]] - 4.0 * product).astype(
            jnp.bfloat16
        )
        if i + 1 < count:
            below = value[:, TILE:] * along[i] - 4.0 * product[:, TILE:]
            coupled[tails[i + 1], tiles[i]] = below.astype(jnp.bfloat16).T
    for i in range(count):
        product = dot(square[tiles[i], :], square[:, tails[i]])
        fourth[tiles[i], tails[i]] = product.astype(jnp.bfloat16)
        rest(fourth, i)
    for i in range(count):
        product = dot(fourth[tiles[i], :], coupled[:, tails[i]])
        value = step[tiles[i], tails[i]].astype(jnp.float32)
        value = ((5.0 * value - product) * 0.25).astype(jnp.bfloat16)
        start = i * TILE
        if start < half:
            root[0, tiles[i], start:half] = value[:, : half - start]
            root[1, tiles[i], :] = value[:, half - start :]
            if start + TILE < half:
                root[0, start + TILE : half, tiles[i]] = value[:, TILE : half - start].T
        else:
            rows, columns = slice(start - half, start - half + TILE), slice(start - half, half)
            root[2, rows, columns] = value
            if start + TILE < width:
                root[2, start - half + TILE : half, rows] = value[:, TILE:].T


def from_left(root, matrix, write):
    half = root.shape[1]
    one, two, three = root[0], root[1], root[2]
    top, bottom = matrix[:half, :], matrix[half:, :]
    write(slice(0, half), slice(None), dot(one, top) + dot(two, bottom))
    write(slice(half, 2 * half), slice(None), dot(two, top, ROWS) + dot(three, bottom))


def from_right(matrix, root, write):
    half = root.shape[1]
    one, two, three = root[0], root[1], root[2]
    before, after = matrix[:, :half], matrix[:, half:]
    write(slice(None), slice(0, half), dot(before, one) + dot(after, two, COLUMNS))
    write(slice(None), slice(half, 2 * half), dot(before, two) + dot(after, three))


def side_kernel(place, root, grad, side, grad_sum):
    core = place[0]

    def write(rows, columns, product):
        side[rows, columns] = product.astype(jnp.bfloat16)

    @pl.when(core == 0)
    def _():
        from_left(root, grad, write)

    @pl.when(core == 1)
    def _():
        from_right(grad, root, write)

    value = grad[...].astype(jnp.float32)
    grad_sum[...] = jnp.sum(value * value, axis=0, keepdims=True)


def finish_kernel(place, own, side, root, grad_sum, out, raw):
    core = place[0]
    half, width = own.shape

    def write(rows, columns, product):
        raw[rows, columns] = product
        square = jnp.sum(product * product, axis=0, keepdims=True)
        sums.append(jnp.sum(square, axis=1, keepdims=True))

    def left():
        sums.clear()
        from_left(root, side, write)
        return sums[0] + sums[1]

    def right():
        sums.clear()
        from_right(side, root, write)
        return sums[0] + sums[1]

    sums = []
    raw_sum = lax.cond(core == 0, right, left)
    scale = 1.0 / (width * width)
    grad_mean = jnp.sum(grad_sum[...], axis=1, keepdims=True) * scale
    raw_mean = jnp.sum(raw_sum, axis=1, keepdims=True) * scale
    ratio = jnp.sqrt(grad_mean + 1e-06) / jnp.sqrt(raw_mean + 1e-06)
    active = place[1] > 0

    @pl.when(active)
    def _():
        out[...] = (raw[rows_at(core * half, half), :] * ratio).astype(jnp.bfloat16)

    @pl.when(jnp.logical_not(active))
    def _():
        out[...] = own[...]


def place_kernel(targets, place, *refs):
    *pieces, out, sems = refs
    core, plane = place[0], place[2]
    copies = []
    for index, (which, skip, count, shift, start, mine) in enumerate(targets):
        rows = pieces[which].shape[1]
        half = core if mine else 1 - core
        first = lax.rem(plane + shift, 4) * (out.shape[0] // 4) + start
        copies.append(
            pltpu.make_async_copy(
                pieces[which].at[pl.ds(skip, count)],
                out.at[pl.ds(first, count), rows_at(half * rows, rows), :],
                sems.at[index],
            )
        )
    for copy in copies:
        copy.start()
    for copy in copies:
        copy.wait()


def local(partials, owned_block):
    core = lax.axis_index("core")
    plane = lax.axis_index("z")
    slot = lax.axis_index("y") * 4 + lax.axis_index("x")
    _, blocks, piece_rows, width = partials.shape
    planes = 4
    per_plane = blocks // planes
    part = per_plane // 2
    rows = piece_rows // 2
    shards = 16
    half = rows * shards
    swap = [(0, 1), (1, 0)]
    up = [(i, (i + 1) % planes) for i in range(planes)]
    down = [(i, (i - 1) % planes) for i in range(planes)]
    def plus(*terms):
        total = terms[0].astype(jnp.float32)
        for term in terms[1:]:
            total = total + term.astype(jnp.float32)
        return total.astype(jnp.bfloat16)

    smem = pl.BlockSpec(memory_space=pltpu.SMEM)
    vmem = pl.BlockSpec(memory_space=pltpu.VMEM)
    anywhere = pl.BlockSpec(memory_space=pl.ANY)
    halves = partials.reshape(planes, per_plane, 2, rows, width)

    def rows_of(here, shift, which):
        sliced = lax.dynamic_slice(
            halves, ((here + shift) % planes, 0, which, 0, 0), (1, per_plane, 1, rows, width)
        )
        return sliced.reshape(per_plane, rows, width)

    with jax.named_scope("sum_over_replicas"):
        sent, next_plane = lax.optimization_barrier((rows_of(plane, 2, 1 - core), plane))
        got = lax.ppermute(sent, "core", swap)
        kept, *sent = lax.optimization_barrier(
            [rows_of(next_plane, 2, core)] + [rows_of(next_plane, k, 1 - core) for k in (1, 3, 0)]
        )
        got_above, got_below, got_mine = (lax.ppermute(each, "core", swap) for each in sent)
        far_low, far_high = pl.pallas_call(
            add_kernel,
            out_shape=[jax.ShapeDtypeStruct((part, rows, width), jnp.bfloat16)] * 2,
            in_specs=[vmem] * 2,
            out_specs=[vmem] * 2,
            compiler_params=pltpu.CompilerParams(vmem_limit_bytes=8 * mib),
            cost_estimate=pl.CostEstimate(
                flops=kept.size, bytes_accessed=6 * kept.size, transcendentals=0
            ),
            name="add_rows",
        )(kept, got)
        far_low, far_high, here = lax.optimization_barrier((far_low, far_high, plane))
        from_above = lax.ppermute(far_low, "z", down)
        from_below = lax.ppermute(far_high, "z", up)
        kept_above, kept_below, kept_mine = lax.optimization_barrier(
            [rows_of(here, k, core) for k in (1, 3, 0)]
        )
        to_above = plus(kept_above, got_above)
        to_below = plus(kept_below, got_below)
        mine = plus(kept_mine, got_mine)
        low_below = lax.ppermute(to_above[:part], "z", up)
        high_above = lax.ppermute(to_below[part:], "z", down)
        low_below, owners = lax.optimization_barrier((low_below, owned_block))
        low_above = lax.ppermute(plus(to_below[:part], from_above), "z", down)
        high_below = lax.ppermute(plus(to_above[part:], from_below), "z", up)
        summed = pl.pallas_call(
            sum_kernel,
            out_shape=jax.ShapeDtypeStruct((shards, rows, width), jnp.bfloat16),
            in_specs=[vmem] * 5,
            out_specs=vmem,
            compiler_params=pltpu.CompilerParams(vmem_limit_bytes=8 * mib),
            cost_estimate=pl.CostEstimate(
                flops=2 * mine.size, bytes_accessed=8 * mine.size, transcendentals=0
            ),
            name="sum_rows",
        )(mine, low_below, low_above, high_above, high_below)

    block = plane * per_plane + slot
    active = jnp.any(owners == block) & (slot < per_plane)
    place = jnp.stack([core, active.astype(jnp.int32), plane]).astype(jnp.int32)
    summed, place = lax.optimization_barrier((summed, place))

    with jax.named_scope("rows_to_owner"):
        own = lax.all_to_all(summed, ("y", "x"), 0, 0, tiled=True).reshape(half, width)
        sibling = lax.ppermute(own, "core", swap)

    square = (width, width)
    whole = jax.ShapeDtypeStruct(square, jnp.bfloat16)
    work = 2 * width**3
    own_root, grad = pl.pallas_call(
        root_kernel,
        out_shape=[jax.ShapeDtypeStruct((3, half, half), jnp.bfloat16), whole],
        in_specs=[smem, vmem, vmem],
        out_specs=[vmem, vmem],
        scratch_shapes=[
            pltpu.VMEM(square, jnp.float32),
        ]
        + [pltpu.VMEM(square, jnp.bfloat16)] * 4,
        compiler_params=pltpu.CompilerParams(vmem_limit_bytes=40 * mib),
        cost_estimate=pl.CostEstimate(flops=3 * work, bytes_accessed=6 * mib, transcendentals=0),
        name="inverse_root",
    )(place, own, sibling)
    sibling_root = lax.ppermute(own_root, "core", swap)
    side, grad_sum = pl.pallas_call(
        side_kernel,
        out_shape=[whole, jax.ShapeDtypeStruct((1, width), jnp.float32)],
        in_specs=[smem, vmem, vmem],
        out_specs=[vmem, vmem],
        compiler_params=pltpu.CompilerParams(vmem_limit_bytes=32 * mib),
        cost_estimate=pl.CostEstimate(flops=work, bytes_accessed=6 * mib, transcendentals=0),
        name="apply_own_root",
    )(place, own_root, grad)
    finished = pl.pallas_call(
        finish_kernel,
        out_shape=jax.ShapeDtypeStruct((half, width), jnp.bfloat16),
        in_specs=[smem, vmem, vmem, vmem, vmem],
        out_specs=vmem,
        scratch_shapes=[pltpu.VMEM(square, jnp.float32)],
        compiler_params=pltpu.CompilerParams(vmem_limit_bytes=32 * mib),
        cost_estimate=pl.CostEstimate(flops=work, bytes_accessed=6 * mib, transcendentals=0),
        name="apply_other_root",
    )(place, own, side, sibling_root, grad_sum)

    with jax.named_scope("rows_to_shards"):
        back = lax.all_to_all(
            finished.reshape(shards, rows, width), ("y", "x"), 0, 0, tiled=True
        )[:per_plane]

    out_shape = jax.ShapeDtypeStruct((blocks, piece_rows, width), jnp.bfloat16)

    def put(name, before, *entries):
        targets, operands = [], []
        for which, (array, *runs) in enumerate(entries):
            skip = 0
            for shift, start, count, mine in runs:
                targets.append((which, skip, count, shift, start, mine))
                skip += count
            operands.append(array)
        moved = sum(4 * operand.size for operand in operands)
        operands.append(before)
        first = before.shape != out_shape.shape
        return pl.pallas_call(
            functools.partial(place_kernel, targets),
            out_shape=out_shape,
            in_specs=[smem] + [vmem] * len(entries) + [vmem if first else anywhere],
            out_specs=anywhere,
            scratch_shapes=[pltpu.SemaphoreType.DMA((len(targets),))],
            input_output_aliases={} if first else {len(operands): 0},
            compiler_params=pltpu.CompilerParams(vmem_limit_bytes=24 * mib),
            cost_estimate=pl.CostEstimate(flops=0, bytes_accessed=moved, transcendentals=0),
            name=name,
        )(place, *operands)

    def other_core(piece):
        return lax.ppermute(piece, "core", swap)

    with jax.named_scope("gather_over_replicas"):
        above_low = lax.ppermute(back[:part], "z", down)
        below_high = lax.ppermute(back[part:], "z", up)
        behind = other_core(back[:1, :16, :128])
        low, high, behind = lax.optimization_barrier((back[:part], back[part:], behind))
        above_high = lax.ppermute(high, "z", down)
        below_low = lax.ppermute(low, "z", up)
        above_low, below_high, other = lax.optimization_barrier(
            (above_low, below_high, other_core(back))
        )
        far_low = lax.ppermute(above_low, "z", down)
        far_high = lax.ppermute(below_high, "z", up)
        passed = other_core(jnp.concatenate([above_low, below_high], axis=0))
        out = put(
            "place_early",
            behind,
            (back, (0, 0, per_plane, True)),
            (other, (0, 0, per_plane, False)),
            (above_low, (1, 0, part, True)),
            (below_high, (3, part, part, True)),
            (above_high, (1, part, part, True)),
            (below_low, (3, 0, part, True)),
        )
        above_high, below_low, out = lax.optimization_barrier((above_high, below_low, out))
        return put(
            "place_late",
            out,
            (passed, (1, 0, part, False), (3, part, part, False)),
            (other_core(above_high), (1, part, part, False)),
            (other_core(below_low), (3, 0, part, False)),
            (far_low, (2, 0, part, True)),
            (far_high, (2, part, part, True)),
            (other_core(far_low), (2, 0, part, False)),
            (other_core(far_high), (2, part, part, False)),
        )


def solution(mesh):
    grid = Mesh(mesh.devices.reshape(4, 2, 4, 4), ("z", "core", "y", "x"))
    in_specs = (P(("z", "core"), None, ("y", "x"), None), P())
    out_specs = P(None, ("y", "x"), None)
    return jax.shard_map(local, mesh=grid, in_specs=in_specs, out_specs=out_specs, check_vma=False)
```

```python
import functools

import jax
import jax.numpy as jnp
from jax import lax
from jax.experimental import pallas as pl
from jax.experimental.pallas import tpu as pltpu
from jax.sharding import Mesh, PartitionSpec as P

damping = 0.1
mib = 2**20
TILE = 256
ROWS = ((0,), (0,))
COLUMNS = ((1,), (1,))


def dot(a, b, contract=((1,), (0,))):
    return lax.dot_general(a, b, (contract, ((), ())), preferred_element_type=jnp.float32)


def rows_at(start, count):
    return pl.ds(pl.multiple_of(start, count), count)


def add_kernel(one, two, *outs):
    start = 0
    for out in outs:
        run = slice(start, start + out.shape[0])
        out[...] = (one[run].astype(jnp.float32) + two[run].astype(jnp.float32)).astype(out.dtype)
        start += out.shape[0]


def sum_kernel(mine, low_below, low_above, high_above, high_below, out):
    count, part = mine.shape[0], low_below.shape[0]
    for run, one, two in (
        (slice(0, part), low_below, low_above),
        (slice(part, count), high_above, high_below),
    ):
        total = mine[run].astype(jnp.float32) + one[...].astype(jnp.float32)
        out[run] = (total + two[...].astype(jnp.float32)).astype(out.dtype)
    out[count:] = jnp.zeros((out.shape[0] - count, *out.shape[1:]), out.dtype)


def root_kernel(place, own, sibling, root, grad, stat, step, square, coupled, fourth):
    core = place[0]
    half, width = own.shape
    grad[rows_at(core * half, half), :] = own[...]
    grad[rows_at((1 - core) * half, half), :] = sibling[...]
    count = width // TILE
    tiles = [slice(i * TILE, (i + 1) * TILE) for i in range(count)]
    tails = [slice(i * TILE, width) for i in range(count)]
    eye = lax.broadcasted_iota(jnp.int32, (TILE, TILE), 0) == lax.broadcasted_iota(
        jnp.int32, (TILE, TILE), 1
    )

    def squares(value):
        return jnp.sum(value * value, axis=0, keepdims=True)

    def add_up(value):
        return jnp.sum(value, axis=1, keepdims=True)

    def statistic(contract):
        total = jnp.zeros((1, 1), jnp.float32)
        for i in range(count):
            if contract == ROWS:
                product = dot(grad[:, tiles[i]], grad[:, tails[i]], ROWS)
            else:
                product = dot(grad[tiles[i], :], grad[tails[i], :], COLUMNS)
            value = product * (1.0 / width)
            block = value[:, :TILE] + jnp.where(eye, damping, 0.0)
            stat[tiles[i], tiles[i]] = block
            total = total + add_up(squares(block))
            if i + 1 < count:
                stat[tiles[i], tails[i + 1]] = value[:, TILE:]
                total = total + 2.0 * add_up(squares(value[:, TILE:]))
        return total

    total = lax.cond(core == 0, lambda: statistic(COLUMNS), lambda: statistic(ROWS))
    inverse = 4.0 * lax.rsqrt(total)

    def rest(matrix, i):
        if i + 1 < count:
            matrix[tails[i + 1], tiles[i]] = matrix[tiles[i], tails[i + 1]].T

    across, along = [], []
    for i in range(count):
        matrix = (stat[tiles[i], tails[i]] * inverse).astype(jnp.bfloat16).astype(jnp.float32)
        block = matrix[:, :TILE]
        value = ((jnp.where(eye, 5.0, 0.0) - block) * 0.25).astype(jnp.bfloat16)
        both = jnp.where(eye, 4.0 * value.astype(jnp.float32) + block, 0.0)
        across.append(jnp.sum(both, axis=0, keepdims=True))
        along.append(jnp.sum(both, axis=1, keepdims=True))
        step[tiles[i], tiles[i]] = value
        if i + 1 < count:
            step[tiles[i], tails[i + 1]] = (matrix[:, TILE:] * -0.25).astype(jnp.bfloat16)
            rest(step, i)
    across = jnp.concatenate(across, axis=1)
    for i in range(count):
        product = dot(step[tiles[i], :], step[:, tails[i]])
        square[tiles[i], tails[i]] = product.astype(jnp.bfloat16)
        rest(square, i)
        value = step[tiles[i], tails[i]].astype(jnp.float32)
        coupled[tiles[i], tails[i]] = (value * across[:, tails[i]] - 4.0 * product).astype(
            jnp.bfloat16
        )
        if i + 1 < count:
            below = value[:, TILE:] * along[i] - 4.0 * product[:, TILE:]
            coupled[tails[i + 1], tiles[i]] = below.astype(jnp.bfloat16).T
    for i in range(count):
        product = dot(square[tiles[i], :], square[:, tails[i]])
        fourth[tiles[i], tails[i]] = product.astype(jnp.bfloat16)
        rest(fourth, i)
    for i in range(count):
        product = dot(fourth[tiles[i], :], coupled[:, tails[i]])
        value = step[tiles[i], tails[i]].astype(jnp.float32)
        value = ((5.0 * value - product) * 0.25).astype(jnp.bfloat16)
        start = i * TILE
        if start < half:
            root[0, tiles[i], start:half] = value[:, : half - start]
            root[1, tiles[i], :] = value[:, half - start :]
            if start + TILE < half:
                root[0, start + TILE : half, tiles[i]] = value[:, TILE : half - start].T
        else:
            rows, columns = slice(start - half, start - half + TILE), slice(start - half, half)
            root[2, rows, columns] = value
            if start + TILE < width:
                root[2, start - half + TILE : half, rows] = value[:, TILE:].T


def from_left(root, matrix, write):
    half = root.shape[1]
    one, two, three = root[0], root[1], root[2]
    top, bottom = matrix[:half, :], matrix[half:, :]
    write(slice(0, half), slice(None), dot(one, top) + dot(two, bottom))
    write(slice(half, 2 * half), slice(None), dot(two, top, ROWS) + dot(three, bottom))


def from_right(matrix, root, write):
    half = root.shape[1]
    one, two, three = root[0], root[1], root[2]
    before, after = matrix[:, :half], matrix[:, half:]
    write(slice(None), slice(0, half), dot(before, one) + dot(after, two, COLUMNS))
    write(slice(None), slice(half, 2 * half), dot(before, two) + dot(after, three))


def side_kernel(place, root, grad, side, grad_sum):
    core = place[0]

    def write(rows, columns, product):
        side[rows, columns] = product.astype(jnp.bfloat16)

    @pl.when(core == 0)
    def _():
        from_left(root, grad, write)

    @pl.when(core == 1)
    def _():
        from_right(grad, root, write)

    value = grad[...].astype(jnp.float32)
    grad_sum[...] = jnp.sum(value * value, axis=0, keepdims=True)


def finish_kernel(place, own, side, root, grad_sum, out, raw):
    core = place[0]
    half, width = own.shape

    def write(rows, columns, product):
        raw[rows, columns] = product
        square = jnp.sum(product * product, axis=0, keepdims=True)
        sums.append(jnp.sum(square, axis=1, keepdims=True))

    def left():
        sums.clear()
        from_left(root, side, write)
        return sums[0] + sums[1]

    def right():
        sums.clear()
        from_right(side, root, write)
        return sums[0] + sums[1]

    sums = []
    raw_sum = lax.cond(core == 0, right, left)
    scale = 1.0 / (width * width)
    grad_mean = jnp.sum(grad_sum[...], axis=1, keepdims=True) * scale
    raw_mean = jnp.sum(raw_sum, axis=1, keepdims=True) * scale
    ratio = jnp.sqrt(grad_mean + 1e-06) / jnp.sqrt(raw_mean + 1e-06)
    active = place[1] > 0

    @pl.when(active)
    def _():
        out[...] = (raw[rows_at(core * half, half), :] * ratio).astype(jnp.bfloat16)

    @pl.when(jnp.logical_not(active))
    def _():
        out[...] = own[...]


def place_kernel(targets, place, *refs):
    *pieces, out, sems = refs
    core, plane = place[0], place[2]
    copies = []
    for index, (which, skip, count, shift, start, mine) in enumerate(targets):
        rows = pieces[which].shape[1]
        half = core if mine else 1 - core
        first = lax.rem(plane + shift, 4) * (out.shape[0] // 4) + start
        copies.append(
            pltpu.make_async_copy(
                pieces[which].at[pl.ds(skip, count)],
                out.at[pl.ds(first, count), rows_at(half * rows, rows), :],
                sems.at[index],
            )
        )
    for copy in copies:
        copy.start()
    for copy in copies:
        copy.wait()


def local(partials, owned_block):
    core = lax.axis_index("core")
    plane = lax.axis_index("z")
    slot = lax.axis_index("y") * 4 + lax.axis_index("x")
    _, blocks, piece_rows, width = partials.shape
    planes = 4
    per_plane = blocks // planes
    part = per_plane // 2
    rows = piece_rows // 2
    shards = 16
    half = rows * shards
    swap = [(0, 1), (1, 0)]
    up = [(i, (i + 1) % planes) for i in range(planes)]
    down = [(i, (i - 1) % planes) for i in range(planes)]
    def plus(*terms):
        total = terms[0].astype(jnp.float32)
        for term in terms[1:]:
            total = total + term.astype(jnp.float32)
        return total.astype(jnp.bfloat16)

    smem = pl.BlockSpec(memory_space=pltpu.SMEM)
    vmem = pl.BlockSpec(memory_space=pltpu.VMEM)
    anywhere = pl.BlockSpec(memory_space=pl.ANY)
    halves = partials.reshape(planes, per_plane, 2, rows, width)

    def rows_of(here, shift, which):
        sliced = lax.dynamic_slice(
            halves, ((here + shift) % planes, 0, which, 0, 0), (1, per_plane, 1, rows, width)
        )
        return sliced.reshape(per_plane, rows, width)

    def add(one, two, runs):
        return pl.pallas_call(
            add_kernel,
            out_shape=[
                jax.ShapeDtypeStruct((one.shape[0] // runs, rows, width), jnp.bfloat16)
            ] * runs,
            in_specs=[vmem] * 2,
            out_specs=[vmem] * runs,
            compiler_params=pltpu.CompilerParams(vmem_limit_bytes=8 * mib),
            cost_estimate=pl.CostEstimate(
                flops=one.size, bytes_accessed=6 * one.size, transcendentals=0
            ),
            name="add_rows",
        )(one, two)

    with jax.named_scope("sum_over_replicas"):
        sent, next_plane = lax.optimization_barrier((rows_of(plane, 2, 1 - core), plane))
        got = lax.ppermute(sent, "core", swap)
        kept, *sent = lax.optimization_barrier(
            [rows_of(next_plane, 2, core)] + [rows_of(next_plane, k, 1 - core) for k in (1, 3, 0)]
        )
        got_above, got_below, got_mine = (lax.ppermute(each, "core", swap) for each in sent)
        far_low, far_high = add(kept, got, 2)
        far_low, far_high, here = lax.optimization_barrier((far_low, far_high, plane))
        from_above = lax.ppermute(far_low, "z", down)
        from_below = lax.ppermute(far_high, "z", up)
        kept_above, kept_below, kept_mine = lax.optimization_barrier(
            [rows_of(here, k, core) for k in (1, 3, 0)]
        )
        to_above = plus(kept_above, got_above)
        to_below = plus(kept_below, got_below)
        mine = plus(kept_mine, got_mine)
        low_below = lax.ppermute(to_above[:part], "z", up)
        high_above = lax.ppermute(to_below[part:], "z", down)
        low_below, owners = lax.optimization_barrier((low_below, owned_block))
        low_above = lax.ppermute(*add(to_below[:part], from_above, 1), "z", down)
        high_below = lax.ppermute(*add(to_above[part:], from_below, 1), "z", up)
        summed = pl.pallas_call(
            sum_kernel,
            out_shape=jax.ShapeDtypeStruct((shards, rows, width), jnp.bfloat16),
            in_specs=[vmem] * 5,
            out_specs=vmem,
            compiler_params=pltpu.CompilerParams(vmem_limit_bytes=8 * mib),
            cost_estimate=pl.CostEstimate(
                flops=2 * mine.size, bytes_accessed=8 * mine.size, transcendentals=0
            ),
            name="sum_rows",
        )(mine, low_below, low_above, high_above, high_below)

    block = plane * per_plane + slot
    active = jnp.any(owners == block) & (slot < per_plane)
    place = jnp.stack([core, active.astype(jnp.int32), plane]).astype(jnp.int32)
    summed, place = lax.optimization_barrier((summed, place))

    with jax.named_scope("rows_to_owner"):
        own = lax.all_to_all(summed, ("y", "x"), 0, 0, tiled=True).reshape(half, width)
        sibling = lax.ppermute(own, "core", swap)

    square = (width, width)
    whole = jax.ShapeDtypeStruct(square, jnp.bfloat16)
    work = 2 * width**3
    own_root, grad = pl.pallas_call(
        root_kernel,
        out_shape=[jax.ShapeDtypeStruct((3, half, half), jnp.bfloat16), whole],
        in_specs=[smem, vmem, vmem],
        out_specs=[vmem, vmem],
        scratch_shapes=[
            pltpu.VMEM(square, jnp.float32),
        ]
        + [pltpu.VMEM(square, jnp.bfloat16)] * 4,
        compiler_params=pltpu.CompilerParams(vmem_limit_bytes=40 * mib),
        cost_estimate=pl.CostEstimate(flops=3 * work, bytes_accessed=6 * mib, transcendentals=0),
        name="inverse_root",
    )(place, own, sibling)
    sibling_root = lax.ppermute(own_root, "core", swap)
    side, grad_sum = pl.pallas_call(
        side_kernel,
        out_shape=[whole, jax.ShapeDtypeStruct((1, width), jnp.float32)],
        in_specs=[smem, vmem, vmem],
        out_specs=[vmem, vmem],
        compiler_params=pltpu.CompilerParams(vmem_limit_bytes=32 * mib),
        cost_estimate=pl.CostEstimate(flops=work, bytes_accessed=6 * mib, transcendentals=0),
        name="apply_own_root",
    )(place, own_root, grad)
    finished = pl.pallas_call(
        finish_kernel,
        out_shape=jax.ShapeDtypeStruct((half, width), jnp.bfloat16),
        in_specs=[smem, vmem, vmem, vmem, vmem],
        out_specs=vmem,
        scratch_shapes=[pltpu.VMEM(square, jnp.float32)],
        compiler_params=pltpu.CompilerParams(vmem_limit_bytes=32 * mib),
        cost_estimate=pl.CostEstimate(flops=work, bytes_accessed=6 * mib, transcendentals=0),
        name="apply_other_root",
    )(place, own, side, sibling_root, grad_sum)

    with jax.named_scope("rows_to_shards"):
        back = lax.all_to_all(
            finished.reshape(shards, rows, width), ("y", "x"), 0, 0, tiled=True
        )[:per_plane]

    out_shape = jax.ShapeDtypeStruct((blocks, piece_rows, width), jnp.bfloat16)

    def put(name, before, *entries):
        targets, operands = [], []
        for which, (array, *runs) in enumerate(entries):
            skip = 0
            for shift, start, count, mine in runs:
                targets.append((which, skip, count, shift, start, mine))
                skip += count
            operands.append(array)
        moved = sum(4 * operand.size for operand in operands)
        operands.append(before)
        first = before.shape != out_shape.shape
        return pl.pallas_call(
            functools.partial(place_kernel, targets),
            out_shape=out_shape,
            in_specs=[smem] + [vmem] * len(entries) + [vmem if first else anywhere],
            out_specs=anywhere,
            scratch_shapes=[pltpu.SemaphoreType.DMA((len(targets),))],
            input_output_aliases={} if first else {len(operands): 0},
            compiler_params=pltpu.CompilerParams(vmem_limit_bytes=24 * mib),
            cost_estimate=pl.CostEstimate(flops=0, bytes_accessed=moved, transcendentals=0),
            name=name,
        )(place, *operands)

    def other_core(piece):
        return lax.ppermute(piece, "core", swap)

    with jax.named_scope("gather_over_replicas"):
        above_low = lax.ppermute(back[:part], "z", down)
        below_high = lax.ppermute(back[part:], "z", up)
        behind = other_core(back[:1, :16, :128])
        low, high, behind = lax.optimization_barrier((back[:part], back[part:], behind))
        above_high = lax.ppermute(high, "z", down)
        below_low = lax.ppermute(low, "z", up)
        above_low, below_high, other = lax.optimization_barrier(
            (above_low, below_high, other_core(back))
        )
        far_low = lax.ppermute(above_low, "z", down)
        far_high = lax.ppermute(below_high, "z", up)
        passed = other_core(jnp.concatenate([above_low, below_high], axis=0))
        out = put(
            "place_early",
            behind,
            (back, (0, 0, per_plane, True)),
            (other, (0, 0, per_plane, False)),
            (above_low, (1, 0, part, True)),
            (below_high, (3, part, part, True)),
            (above_high, (1, part, part, True)),
            (below_low, (3, 0, part, True)),
        )
        above_high, below_low, out = lax.optimization_barrier((above_high, below_low, out))
        return put(
            "place_late",
            out,
            (passed, (1, 0, part, False), (3, part, part, False)),
            (other_core(above_high), (1, part, part, False)),
            (other_core(below_low), (3, 0, part, False)),
            (far_low, (2, 0, part, True)),
            (far_high, (2, part, part, True)),
            (other_core(far_low), (2, 0, part, False)),
            (other_core(far_high), (2, part, part, False)),
        )


def solution(mesh):
    grid = Mesh(mesh.devices.reshape(4, 2, 4, 4), ("z", "core", "y", "x"))
    in_specs = (P(("z", "core"), None, ("y", "x"), None), P())
    out_specs = P(None, ("y", "x"), None)
    return jax.shard_map(local, mesh=grid, in_specs=in_specs, out_specs=out_specs, check_vma=False)
```
